256 devices in a mesh: rows: 32 (over y, z), feat: 8 (over x, core).
Axes of the slice: x: 4, y: 4, z: 8, core: 2. Of those that a mesh axis runs over, the one named last changes fastest.
Arguments:
- test_cells: bfloat16 [4096, 3072], P('rows', 'feat'), may hold values from -6 to 6
- train_cells: bfloat16 [16384, 3072], P('rows', 'feat'), may hold values from -6 to 6
- train_present: int32 [16, 16384], P('feat', 'rows'), may hold values from 0 to 1, as said below
- retrieved: int32 [32, 16], P('rows'), may hold values from 0 to 255, as said below
- w_query: bfloat16 [192, 192], replicated, may hold values from -0.4375 to 0.4375
- q_gain: float32 [192], replicated, may hold values from 0.75 to 1.25
- w_key: bfloat16 [192, 192], replicated, may hold values from -0.4375 to 0.4375
- k_gain: float32 [192], replicated, may hold values from 0.75 to 1.25
- w_value: bfloat16 [192, 192], replicated, may hold values from -0.4375 to 0.4375
- w_out: bfloat16 [192, 192], replicated, may hold values from -0.4375 to 0.4375
- gain_one: float32 [192], replicated, may hold values from 0.5 to 1.5
- w_up: bfloat16 [192, 768], replicated, may hold values from -0.4375 to 0.4375
- w_down: bfloat16 [768, 192], replicated, may hold values from -0.21875 to 0.21875
- gain_two: float32 [192], replicated, may hold values from 0.5 to 1.5
- cotangent: bfloat16 [4096, 3072], P('rows', 'feat'), may hold values from -6 to 6
Outputs:
- out_cells: bfloat16 [4096, 3072], P('rows', 'feat')
- grad_test: bfloat16 [4096, 3072], P('rows', 'feat')
- grad_train: bfloat16 [16384, 3072], P('rows', 'feat')
- grad_query: float32 [192, 192], replicated
- grad_key: float32 [192, 192], replicated
- grad_value: float32 [192, 192], replicated
- grad_out: float32 [192, 192], replicated
- grad_up: float32 [192, 768], replicated
- grad_down: float32 [768, 192], replicated
The draws below stay inside these ranges and needn't reach their ends.
Inputs may be any that keep to these rules, and one draw needn't show every extreme that they name: `retrieved`: row b lists 16 distinct train blocks (block g is train rows g * 64 to g * 64 + 63). Call blocks o * 8 to o * 8 + 7 the blocks of row group o: row b takes from every row group either no block or exactly 1, and it always takes 1 block of row group b, among them block b * 8 + 7. `train_present`: 1 marks a present cell, 0 a missing one. For every feature, every train block holds at least one present cell.
All inputs are finite; a program needn't handle non-finite values.
Results may differ from the reference program's by a relative error of at most 0.019.
Values may be sent and summed in bfloat16 or wider, within the bound.
No kernel may reach another device: no remote copies, remote signals or barrier semaphores. Data moves between devices by JAX's collectives and lax.ppermute only.
A program may use at most 128 MiB of HBM per device.

```python
import math
import jax
import jax.numpy as jnp
from jax import lax

E = 192
H = 6
FFH = 768
BLK = 64
R = 16
TB_DEV = 8
TEST_DEV = 128
CAP = 1
OWNERS = 32
FEATURES = 16
TESTS = 4096
TRAINS = 16384


def draw_retrieved(key, part):
    key = jax.random.fold_in(key, 11)
    keys = jax.random.split(key, 4)
    used = R // CAP
    groups = jnp.arange(OWNERS, dtype=jnp.int32)
    popularity = jax.random.randint(keys[0], (OWNERS,), 1, 9)
    score = jax.random.randint(keys[1], (OWNERS, OWNERS), 0, 1 << 16) * popularity[None, :]
    score = jnp.where(groups[:, None] == groups[None, :], 9 << 16, score)
    score = score * OWNERS + groups[None, :]
    _, chosen_groups = lax.top_k(score, used)
    chosen_groups = chosen_groups.astype(jnp.int32)
    block_pop = jax.random.randint(keys[2], (OWNERS * TB_DEV,), 1, 9)
    local = jnp.arange(TB_DEV, dtype=jnp.int32)
    block_ids = chosen_groups[:, :, None] * TB_DEV + local[None, None, :]
    block_score = jax.random.randint(keys[3], (OWNERS, used, TB_DEV), 0, 1 << 16) * jnp.take(block_pop, block_ids)
    forced = (chosen_groups[:, :, None] == groups[:, None, None]) & (local[None, None, :] == TB_DEV - 1)
    block_score = jnp.where(forced, 9 << 16, block_score) * TB_DEV + local[None, None, :]
    _, chosen_local = lax.top_k(block_score, CAP)
    result = chosen_groups[:, :, None] * TB_DEV + chosen_local.astype(jnp.int32)
    return result.reshape(OWNERS, R).astype(jnp.int32)


def draw_train_present(key, part):
    key = jax.random.fold_in(key, 23)
    keys = jax.random.split(key, 3)
    level = jax.random.randint(keys[0], (FEATURES, 1), 1, 9)
    present = jax.random.randint(keys[1], (FEATURES, TRAINS), 0, 16) >= level
    forced = jax.random.randint(keys[2], (FEATURES, TRAINS // BLK, 1), 0, BLK)
    spot = jnp.arange(BLK, dtype=jnp.int32)[None, None, :] == forced
    return (present | spot.reshape(FEATURES, TRAINS)).astype(jnp.int32)


def steps_of(rng, dims, shards, smallest, high):
    level = 1.0
    for position, shards_of in shards:
        steps = jax.random.uniform(jax.random.fold_in(jax.random.fold_in(rng, 6), position), (shards_of,), jnp.float32, smallest / len(shards), high / len(shards))
        level = level * jnp.repeat(jnp.exp(steps), dims[position] // shards_of).reshape((-1,) + (1,) * (len(dims) - 1 - position))
    return level


def scatter_about(key, shape, spread, reach, cuts=(), held_as=jnp.bfloat16):
    entries = jax.random.normal(key, shape, jnp.float32) * spread
    if len(cuts) > 0:
        entries = steps_of(key, shape, cuts, -0.22, 0.18) * entries
    return jnp.clip(entries, min=-reach, max=reach).astype(held_as)


def setup_inputs(seed: int = 0) -> dict:
    splits = jax.random.split(jax.random.key(seed), 16)
    test_cells = scatter_about(splits[0], (TESTS, FEATURES * E), 1.0, 6.0, ((0, 32), (1, 8)))
    train_cells = scatter_about(splits[1], (TRAINS, FEATURES * E), 1.0, 6.0, ((0, 32), (1, 8)))
    train_present = draw_train_present(jax.random.fold_in(splits[15], 71), 0)
    retrieved = draw_retrieved(jax.random.fold_in(splits[15], 71), 0)
    w_query = scatter_about(splits[4], (E, E), E ** -0.5, 0.4375)
    q_gain = jnp.clip(1.0 + 0.05 * jax.random.normal(splits[5], (E,), jnp.float32), 0.75, 1.25)
    w_key = scatter_about(splits[6], (E, E), E ** -0.5, 0.4375)
    k_gain = jnp.clip(1.0 + 0.05 * jax.random.normal(splits[7], (E,), jnp.float32), 0.75, 1.25)
    w_value = scatter_about(splits[8], (E, E), E ** -0.5, 0.4375)
    w_out = scatter_about(splits[9], (E, E), E ** -0.5, 0.4375)
    gain_one = jnp.clip(1.0 + 0.1 * jax.random.normal(splits[10], (E,), jnp.float32), 0.5, 1.5)
    w_up = scatter_about(splits[11], (E, FFH), E ** -0.5, 0.4375)
    w_down = scatter_about(splits[12], (FFH, E), FFH ** -0.5, 0.21875)
    gain_two = jnp.clip(1.0 + 0.1 * jax.random.normal(splits[13], (E,), jnp.float32), 0.5, 1.5)
    cotangent = scatter_about(splits[14], (TESTS, FEATURES * E), 1.0, 6.0, ((0, 32), (1, 8)))
    return dict(test_cells=test_cells, train_cells=train_cells, train_present=train_present, retrieved=retrieved, w_query=w_query, q_gain=q_gain, w_key=w_key, k_gain=k_gain, w_value=w_value, w_out=w_out, gain_one=gain_one, w_up=w_up, w_down=w_down, gain_two=gain_two, cotangent=cotangent)


SCORE_TEMPER = 1.5

def rounded(value):
    return lax.optimization_barrier(value.astype(jnp.bfloat16))

def rms_scale(pre, gain):
    return pre * lax.rsqrt(lax.optimization_barrier(jnp.mean(pre * pre, axis=-1, keepdims=True)) + 1e-06) * gain

def layer_scale(pre, gain):
    centred = pre - lax.optimization_barrier(jnp.mean(pre, axis=-1, keepdims=True))
    return centred * lax.rsqrt(lax.optimization_barrier(jnp.mean(centred * centred, axis=-1, keepdims=True)) + 1e-05) * gain

def project_norm(cells, weight, gain):
    pre = jnp.dot(cells, weight, preferred_element_type=jnp.float32)
    return (pre, rounded(rms_scale(pre, gain)))

def project_back(cells, weight, gain, pre, d_normed):
    _, back = jax.vjp(lambda inner: rms_scale(inner, gain), pre)
    d_pre, = back(d_normed)
    d_pre = rounded(d_pre)
    grad_weight = jnp.dot(cells.T, d_pre, preferred_element_type=jnp.float32)
    d_cells = jnp.dot(d_pre, weight.T, preferred_element_type=jnp.float32)
    return (grad_weight, d_cells)

def head_side(query_cells, attended, w_out, gain_one, w_up, w_down, gain_two, cotangent):
    inner_one = query_cells.astype(jnp.float32) + jnp.dot(attended, w_out, preferred_element_type=jnp.float32)
    normed_one, back_one = jax.vjp(lambda inner: layer_scale(inner, gain_one), inner_one)
    normed_one = rounded(normed_one)
    hidden_pre = jnp.dot(normed_one, w_up, preferred_element_type=jnp.float32)
    hidden, back_gelu = jax.vjp(jax.nn.gelu, hidden_pre)
    hidden = rounded(hidden)
    inner_two = normed_one.astype(jnp.float32) + jnp.dot(hidden, w_down, preferred_element_type=jnp.float32)
    result, back_two = jax.vjp(lambda inner: layer_scale(inner, gain_two), inner_two)
    output = rounded(result)
    d_two, = back_two(cotangent.astype(jnp.float32))
    d_two_b = rounded(d_two)
    grad_down = jnp.dot(hidden.T, d_two_b, preferred_element_type=jnp.float32)
    d_pre, = back_gelu(jnp.dot(d_two_b, w_down.T, preferred_element_type=jnp.float32))
    d_pre_b = rounded(d_pre)
    grad_up = jnp.dot(normed_one.T, d_pre_b, preferred_element_type=jnp.float32)
    d_normed = d_two + jnp.dot(d_pre_b, w_up.T, preferred_element_type=jnp.float32)
    d_one, = back_one(d_normed)
    d_one_b = rounded(d_one)
    grad_out = jnp.dot(attended.T, d_one_b, preferred_element_type=jnp.float32)
    d_attended = rounded(jnp.dot(d_one_b, w_out.T, preferred_element_type=jnp.float32))
    return (output, d_one, d_attended, grad_out, grad_up, grad_down)

def feature_probs(query, key, present, heads):
    rows = query.shape[0]
    count = key.shape[0]
    size = query.shape[1] // heads
    q_part = query.reshape(rows, heads, size).astype(jnp.float32)
    k_part = key.reshape(count, heads, size).astype(jnp.float32)
    scores = jnp.einsum('thd,khd->htk', q_part, k_part) * (SCORE_TEMPER / math.sqrt(size))
    weights = jnp.exp(scores) * present.astype(jnp.float32)
    return weights / lax.optimization_barrier(jnp.sum(weights, axis=-1, keepdims=True))

def feature_forward(query, key, value, present, heads):
    rows = query.shape[0]
    count = key.shape[0]
    size = query.shape[1] // heads
    probs = feature_probs(query, key, present, heads)
    weights = rounded(probs).astype(jnp.float32)
    v_part = value.reshape(count, heads, size).astype(jnp.float32)
    mixed = jnp.einsum('htk,khd->thd', weights, v_part)
    return rounded(mixed.reshape(rows, heads * size))

def feature_back(query, key, value, present, d_att, heads):
    rows = query.shape[0]
    count = key.shape[0]
    size = query.shape[1] // heads
    probs = feature_probs(query, key, present, heads)
    weights = rounded(probs).astype(jnp.float32)
    q_part = query.reshape(rows, heads, size).astype(jnp.float32)
    k_part = key.reshape(count, heads, size).astype(jnp.float32)
    v_part = value.reshape(count, heads, size).astype(jnp.float32)
    g_part = d_att.reshape(rows, heads, size).astype(jnp.float32)
    grad_w = jnp.einsum('thd,khd->htk', g_part, v_part)
    d_scores = probs * (grad_w - lax.optimization_barrier(jnp.sum(probs * grad_w, axis=-1, keepdims=True)))
    d_scores = rounded(d_scores * (SCORE_TEMPER / math.sqrt(size))).astype(jnp.float32)
    d_query = jnp.einsum('htk,khd->thd', d_scores, k_part).reshape(rows, heads * size)
    d_key = rounded(jnp.einsum('htk,thd->khd', d_scores, q_part).reshape(count, heads * size))
    d_value = rounded(jnp.einsum('htk,thd->khd', weights, g_part).reshape(count, heads * size))
    return (d_query, d_key, d_value)

def reference(test_cells, train_cells, train_present, retrieved, w_query, q_gain, w_key, k_gain, w_value, w_out, gain_one, w_up, w_down, gain_two, cotangent):
    width = w_query.shape[0]
    query_cells = test_cells.reshape(-1, width)
    key_cells = train_cells.reshape(-1, width)
    query_pre, query_norm = project_norm(query_cells, w_query, q_gain)
    key_pre, key_norm = project_norm(key_cells, w_key, k_gain)
    values = rounded(jnp.dot(key_cells, w_value, preferred_element_type=jnp.float32))
    query_grid = query_norm.reshape(TESTS, FEATURES, width)
    key_grid = key_norm.reshape(TRAINS, FEATURES, width)
    value_grid = values.reshape(TRAINS, FEATURES, width)
    offsets = jnp.arange(BLK, dtype=jnp.int32)

    def block_inputs(block):
        ids = retrieved[block].astype(jnp.int32)
        key_rows = (ids[:, None] * BLK + offsets[None, :]).reshape(-1).astype(jnp.int32)
        keys = jnp.moveaxis(jnp.take(key_grid, key_rows, axis=0), 1, 0)
        vals = jnp.moveaxis(jnp.take(value_grid, key_rows, axis=0), 1, 0)
        present = jnp.take(train_present, key_rows, axis=1)
        start = (block * TEST_DEV).astype(jnp.int32)
        queries = jnp.moveaxis(lax.dynamic_slice_in_dim(query_grid, start, TEST_DEV, 0), 1, 0)
        return (key_rows, queries, keys, vals, present, start)

    def forward_block(block):
        key_rows, queries, keys, vals, present, start = block_inputs(block)
        return lax.map(lambda items: feature_forward(items[0], items[1], items[2], items[3], H), (queries, keys, vals, present))
    blocks = jnp.arange(OWNERS, dtype=jnp.int32)
    attended = lax.map(forward_block, blocks)
    attended = jnp.transpose(attended, (0, 2, 1, 3)).reshape(-1, width)
    output, d_one, d_att, g_out, g_up, g_down = head_side(query_cells, attended, w_out, gain_one, w_up, w_down, gain_two, cotangent.reshape(-1, width))
    d_att_grid = d_att.reshape(TESTS, FEATURES, width)

    def backward_block(carry, block):
        key_acc, value_acc = carry
        key_rows, queries, keys, vals, present, start = block_inputs(block)
        grads = jnp.moveaxis(lax.dynamic_slice_in_dim(d_att_grid, start, TEST_DEV, 0), 1, 0)
        d_query, d_key, d_value = lax.map(lambda items: feature_back(items[0], items[1], items[2], items[3], items[4], H), (queries, keys, vals, present, grads))
        key_acc = key_acc.at[key_rows].add(jnp.moveaxis(d_key, 0, 1).astype(jnp.float32))
        value_acc = value_acc.at[key_rows].add(jnp.moveaxis(d_value, 0, 1).astype(jnp.float32))
        return ((key_acc, value_acc), jnp.moveaxis(d_query, 0, 1))
    empty = jnp.zeros((TRAINS, FEATURES, width), jnp.float32)
    (key_acc, value_acc), d_query = lax.scan(backward_block, (empty, empty), blocks)
    d_query = d_query.reshape(-1, width)
    g_query, d_qcells = project_back(query_cells, w_query, q_gain, query_pre, d_query)
    grad_test = rounded(d_one + d_qcells).reshape(TESTS, FEATURES * width)
    key_total = rounded(key_acc.reshape(-1, width))
    value_total = rounded(value_acc.reshape(-1, width))
    g_key, d_kcells = project_back(key_cells, w_key, k_gain, key_pre, key_total.astype(jnp.float32))
    g_value = jnp.dot(key_cells.T, value_total, preferred_element_type=jnp.float32)
    d_vcells = jnp.dot(value_total, w_value.T, preferred_element_type=jnp.float32)
    grad_train = rounded(d_kcells + d_vcells).reshape(TRAINS, FEATURES * width)
    out_cells = output.reshape(TESTS, FEATURES * width)
    return (out_cells, grad_test, grad_train, g_query, g_key, g_value, g_out, g_up, g_down)
```

```python
import functools
import math

import jax
import jax.numpy as jnp
from jax import lax
from jax.experimental import pallas as pl
from jax.experimental.pallas import tpu as pltpu
from jax.sharding import PartitionSpec as P

H = 6
BLK = 64
E = 192
W = 256
FFH = 768
SIZE = E // H
TEMPER = 1.5 / math.sqrt(SIZE)
LOG2E = math.log2(math.e)
GELU_C = math.sqrt(2.0 / math.pi)
ABSENT = 8.0
ABSENT_ABOVE = 7.0
MASKED = -30000.0
GRAD_ROWS = 4096

bf16 = jnp.bfloat16
f32 = jnp.float32


def dot_nn(a, b):
    return lax.dot_general(a, b, (((1,), (0,)), ((), ())), preferred_element_type=f32)


def dot_nt(a, b):
    return lax.dot_general(a, b, (((1,), (1,)), ((), ())), preferred_element_type=f32)


def dot_tn(a, b):
    return lax.dot_general(a, b, (((0,), (0,)), ((), ())), preferred_element_type=f32)


def pick_kernel(pick_ref, cells_ref, out_ref):
    def body(slot, carry):
        out_ref[slot] = cells_ref[pick_ref[slot]]
        return carry

    lax.fori_loop(0, out_ref.shape[0], body, 0)


def sum_kernel(asked_ref, back_ref, out_ref, acc_ref):
    acc_ref[...] = jnp.zeros_like(acc_ref)

    def body(slot, carry):
        asked = asked_ref[slot]

        @pl.when(asked >= 0)
        def _():
            acc_ref[asked] += back_ref[slot].astype(f32)

        return carry

    lax.fori_loop(0, back_ref.shape[0], body, 0)
    out_ref[...] = acc_ref[...].astype(bf16)


def mean_e(x):
    return jnp.sum(x, axis=-1, keepdims=True) * (1.0 / E)


def head_blocks(full):
    return jnp.concatenate(
        [full[SIZE * h : SIZE * (h + 1), 128 * h : 128 * (h + 1)] for h in range(H)]
        + [jnp.zeros((W - E, 128), f32)],
        axis=0,
    )


def spread_columns(tall, last):
    row = lax.broadcasted_iota(jnp.int32, tall.shape, 0)
    parts = []
    for h in range(H):
        inside = (row >= SIZE * h) & (row < SIZE * (h + 1))
        part = jnp.where(inside, tall, 0.0)
        if last:
            part = jnp.where(row == E, 1.0, part)
        parts.append(part)
    return jnp.concatenate(parts, axis=1).astype(bf16)


def spread_rows(wide):
    lane = lax.broadcasted_iota(jnp.int32, wide.shape, 1)
    parts = []
    for h in range(H):
        inside = (lane >= SIZE * h) & (lane < SIZE * (h + 1))
        parts.append(jnp.where(inside, wide, 0.0))
    return jnp.concatenate(parts, axis=0).astype(bf16)


def layer_norm(x, lane_in):
    centred = jnp.where(lane_in, x - mean_e(x), 0.0)
    scale = lax.rsqrt(mean_e(centred * centred) + 1e-05)
    return centred * scale, scale


def layer_norm_back(hat, scale, gain, dy):
    u = dy * gain
    return scale * (u - mean_e(u) - hat * mean_e(u * hat))


def rms_back(pre, scale, gain, dy):
    u = dy * gain
    return scale * (u - pre * (scale * scale) * mean_e(pre * u))


def main_kernel(
    chunk,
    owner_ref,
    rec_ref,
    test_ref,
    cot_ref,
    wq_ref,
    wk_ref,
    wv_ref,
    place_ref,
    wqt_ref,
    wkt_ref,
    wvt_ref,
    placet_ref,
    w_out_ref,
    w_up_ref,
    w_down_ref,
    gains_ref,
    out_ref,
    grad_test_ref,
    send_ref,
    grads_ref,
    cells_s,
    kp_s,
    k_s,
    v_s,
    e_s,
    p_s,
    d_s,
):
    count = owner_ref.shape[0]
    feats = 2
    rows = test_ref.shape[0]
    keys = count * BLK
    chunks = keys // chunk
    q_gain = gains_ref[0:1, :]
    k_gain = gains_ref[1:2, :]
    gain_one = gains_ref[2:3, :]
    gain_two = gains_ref[3:4, :]

    def gather(j, carry):
        cells_s[pl.ds(pl.multiple_of(j * BLK, BLK), BLK), :] = rec_ref[owner_ref[j]]
        return carry

    lax.fori_loop(0, count, gather, 0)

    test = test_ref[...]
    tc, qp, qr, qn, qt = [], [], [], [], []
    for f in range(feats):
        pre = dot_nn(test, wq_ref[f])
        scale = lax.rsqrt(mean_e(pre * pre) + 1e-06)
        norm = pre * scale * q_gain
        norm = norm.astype(bf16).astype(f32)
        tc.append(dot_nn(test, place_ref[f]))
        qp.append(pre)
        qr.append(scale)
        qn.append(norm)
        qt.append(spread_columns(norm.T, True))

    def scores(c, totals):
        start = pl.ds(pl.multiple_of(c * chunk, chunk), chunk)
        cells = cells_s[start, :]
        result = []
        for f in range(feats):
            pre = dot_nn(cells, wk_ref[f])
            lane = lax.broadcasted_iota(jnp.int32, pre.shape, 1)
            body = jnp.where(lane < E, pre, 0.0)
            scale = lax.rsqrt(mean_e(body * body) + 1e-06)
            norm = body * scale * k_gain
            bias = jnp.where((lane == E) & (pre > ABSENT_ABOVE), MASKED, 0.0)
            norm = (norm + bias).astype(bf16)
            kp_s[f, start, :] = body
            k_s[f, start, :] = norm
            v_s[f, start, :] = dot_nn(cells, wv_ref[f]).astype(bf16)
            e = jnp.exp2(dot_nn(norm, qt[f]) * (TEMPER * LOG2E))
            e_s[f, start, :] = e
            result.append(totals[f] + jnp.sum(e, axis=0, keepdims=True))
        return tuple(result)

    zero = jnp.zeros((1, H * rows), f32)
    totals = lax.fori_loop(0, chunks, scores, (zero,) * feats)
    inverse = [1.0 / total for total in totals]

    def attend(c, mixed):
        start = pl.ds(pl.multiple_of(c * chunk, chunk), chunk)
        result = []
        for f in range(feats):
            p = (e_s[f, start, :] * inverse[f]).astype(bf16)
            p_s[f, start, :] = p
            result.append(mixed[f] + dot_tn(v_s[f, start, :], p))
        return tuple(result)

    mixed = lax.fori_loop(0, chunks, attend, (jnp.zeros((W, H * rows), f32),) * feats)
    attended_t = [head_blocks(m) for m in mixed]

    attended = jnp.concatenate([a.T for a in attended_t], axis=0).astype(bf16)
    lane_in = lax.broadcasted_iota(jnp.int32, (feats * rows, W), 1) < E
    cells_f32 = jnp.concatenate(tc, axis=0)
    w_out = w_out_ref[...]
    w_up = w_up_ref[...]
    w_down = w_down_ref[...]
    inner_one = cells_f32 + dot_nn(attended, w_out)
    hat_one, scale_one = layer_norm(inner_one, lane_in)
    normed_one = (hat_one * gain_one).astype(bf16)
    pre = dot_nn(normed_one, w_up)
    tanh = jnp.tanh(GELU_C * (pre + 0.044715 * (pre * pre * pre)))
    hidden = (0.5 * pre * (1.0 + tanh)).astype(bf16)
    slope = 0.5 * (1.0 + tanh) + (0.5 * GELU_C) * pre * (1.0 - tanh * tanh) * (
        1.0 + (3 * 0.044715) * (pre * pre)
    )
    inner_two = normed_one.astype(f32) + dot_nn(hidden, w_down)
    hat_two, scale_two = layer_norm(inner_two, lane_in)
    out = (hat_two * gain_two).astype(bf16)
    out_ref[...] = (
        dot_nn(out[:rows], placet_ref[0]) + dot_nn(out[rows:], placet_ref[1])
    ).astype(bf16)
    cot_in = cot_ref[...]
    cot = jnp.concatenate([dot_nn(cot_in, place_ref[f]) for f in range(feats)], axis=0)
    d_two = layer_norm_back(hat_two, scale_two, gain_two, cot)
    d_two = jnp.where(lane_in, d_two, 0.0)
    d_two_b = d_two.astype(bf16)
    d_pre_b = (dot_nt(d_two_b, w_down) * slope).astype(bf16)
    d_normed = d_two + dot_nt(d_pre_b, w_up)
    d_one = layer_norm_back(hat_one, scale_one, gain_one, d_normed)
    d_one = jnp.where(lane_in, d_one, 0.0)
    d_one_b = d_one.astype(bf16)
    d_att = dot_nt(d_one_b, w_out).astype(bf16).astype(f32)
    put_grads(grads_ref, 6, dot_tn(attended, d_one_b)[:E])
    put_grads(grads_ref, 8, dot_tn(normed_one, d_pre_b)[:E])
    put_grads(grads_ref, 14, dot_tn(d_two_b, hidden)[:E])

    da_t, da_rows, q_rows, dots = [], [], [], []
    for f in range(feats):
        mine = d_att[f * rows : (f + 1) * rows]
        mine_t = mine.T
        da_t.append(spread_columns(mine_t, False))
        da_rows.append(spread_rows(mine))
        q_rows.append(spread_rows(qn[f]))
        product = mine_t * attended_t[f]
        dots.append(
            jnp.concatenate(
                [
                    jnp.sum(product[SIZE * h : SIZE * (h + 1)], axis=0, keepdims=True)
                    for h in range(H)
                ],
                axis=1,
            )
        )

    send_ref[...] = jnp.zeros_like(send_ref)

    def back(c, d_queries):
        start = pl.ds(pl.multiple_of(c * chunk, chunk), chunk)
        result = []
        d_cells = jnp.zeros((chunk, feats * E), f32)
        for f in range(feats):
            grad_w = dot_nn(v_s[f, start, :], da_t[f])
            probs = e_s[f, start, :] * inverse[f]
            d_scores = (probs * (grad_w - dots[f]) * TEMPER).astype(bf16)
            result.append(d_queries[f] + dot_tn(k_s[f, start, :], d_scores))
            d_key = dot_nn(d_scores, q_rows[f])
            d_value = dot_nn(p_s[f, start, :], da_rows[f]).astype(bf16)
            body = kp_s[f, start, :]
            scale = lax.rsqrt(mean_e(body * body) + 1e-06)
            d_kpre = rms_back(body, scale, k_gain, d_key).astype(bf16)
            d_s[start, 2 * f * W : (2 * f + 1) * W] = d_kpre
            d_s[start, (2 * f + 1) * W : (2 * f + 2) * W] = d_value
            d_cells = d_cells + dot_nn(d_kpre, wkt_ref[f]) + dot_nn(d_value, wvt_ref[f])
        d_cells = d_cells.astype(bf16)
        for b in range(chunk // BLK):
            send_ref[owner_ref[c * (chunk // BLK) + b]] = d_cells[b * BLK : (b + 1) * BLK]
        return tuple(result)

    d_queries = lax.fori_loop(0, chunks, back, (jnp.zeros((W, H * rows), f32),) * feats)

    d_test = jnp.zeros((rows, feats * E), f32)
    g_query = jnp.zeros((W, W), f32)
    placed = []
    for f in range(feats):
        d_query = head_blocks(d_queries[f]).T
        d_qpre = rms_back(qp[f], qr[f], q_gain, d_query).astype(bf16)
        g_query = g_query + dot_tn(tc[f].astype(bf16), d_qpre)
        d_one_f = d_one[f * rows : (f + 1) * rows]
        d_test = d_test + dot_nn(d_qpre, wqt_ref[f])
        placed.append(d_one_f[:, :E])
    grad_test_ref[...] = (d_test + jnp.concatenate(placed, axis=1)).astype(bf16)
    put_grads(grads_ref, 0, g_query[:E])
    kv = dot_tn(cells_s[...], d_s[...])
    put_grads(grads_ref, 2, kv[:E, : 2 * W] + kv[E:, 2 * W :])
    grads_ref[20 * E :, :] = jnp.zeros((GRAD_ROWS - 20 * E, 128), bf16)


def put_grads(grads_ref, first, value):
    for i in range(value.shape[1] // 128):
        rows = slice((first + i) * E, (first + i + 1) * E)
        grads_ref[rows, :] = value[:, 128 * i : 128 * (i + 1)].astype(bf16)


def take_grads(ref, first, pieces):
    return jnp.concatenate(
        [ref[(first + i) * E : (first + i + 1) * E, :].astype(f32) for i in range(pieces)], axis=1
    )


def add_kernel(in_ref, out_ref):
    out_ref[...] = jnp.sum(in_ref[...].astype(f32), axis=0).astype(bf16)


def add_copies_kernel(in_ref, out_ref):
    total = jnp.sum(in_ref[...].astype(f32), axis=0).astype(bf16)
    out_ref[...] = jnp.broadcast_to(total[None], out_ref.shape)


def unpack_kernel(in_ref, query_ref, key_ref, value_ref, w_out_ref, up_ref, down_ref):
    for i, ref in enumerate((query_ref, key_ref, value_ref, w_out_ref)):
        ref[...] = take_grads(in_ref, 2 * i, 2)[:, :E]
    up_ref[...] = take_grads(in_ref, 8, 6)
    down_ref[...] = take_grads(in_ref, 14, 6).T


def vmem_specs(n):
    return [pl.BlockSpec(memory_space=pltpu.VMEM)] * n


SMEM_SPEC = pl.BlockSpec(memory_space=pltpu.SMEM)
LIMIT = 48 * 1024 * 1024


def main_call(owner_of, rec, test_cells, cotangent, weights, chunk):
    count = owner_of.shape[0]
    keys = count * BLK
    rows, wide = test_cells.shape
    ht = H * rows
    return pl.pallas_call(
        functools.partial(main_kernel, chunk),
        out_shape=(
            jax.ShapeDtypeStruct((rows, wide), bf16),
            jax.ShapeDtypeStruct((rows, wide), bf16),
            jax.ShapeDtypeStruct(rec.shape, bf16),
            jax.ShapeDtypeStruct((GRAD_ROWS, 128), bf16),
        ),
        in_specs=[SMEM_SPEC] + vmem_specs(3 + len(weights)),
        out_specs=tuple(vmem_specs(4)),
        scratch_shapes=[
            pltpu.VMEM((keys, wide), bf16),
            pltpu.VMEM((2, keys, W), f32),
            pltpu.VMEM((2, keys, W), bf16),
            pltpu.VMEM((2, keys, W), bf16),
            pltpu.VMEM((2, keys, ht), f32),
            pltpu.VMEM((2, keys, ht), bf16),
            pltpu.VMEM((keys, 4 * W), bf16),
        ],
        compiler_params=pltpu.CompilerParams(vmem_limit_bytes=LIMIT),
    )(owner_of, rec, test_cells, cotangent, *weights)


def pad_to(x, rows, cols):
    return jnp.pad(x, ((0, rows - x.shape[0]), (0, cols - x.shape[1])))


def prepare(w_query, q_gain, w_key, k_gain, w_value, w_out, gain_one, w_up, w_down, gain_two):
    def at_feature(w):
        zero = jnp.zeros_like(w)
        return jnp.stack([jnp.concatenate([w, zero]), jnp.concatenate([zero, w])])

    def turned(w):
        t = pad_to(w.T, W, E)
        zero = jnp.zeros_like(t)
        return jnp.stack(
            [jnp.concatenate([t, zero], axis=1), jnp.concatenate([zero, t], axis=1)]
        )

    eye = jnp.eye(E, dtype=bf16)
    first = jnp.zeros((E, W), bf16).at[0, E].set(1.0)
    gains = jnp.stack([jnp.pad(g, (0, W - E)) for g in (q_gain, k_gain, gain_one, gain_two)])
    return (
        at_feature(pad_to(w_query, E, W)),
        at_feature(pad_to(w_key, E, W) + first),
        at_feature(pad_to(w_value, E, W)),
        at_feature(pad_to(eye, E, W)),
        turned(w_query),
        turned(w_key),
        turned(w_value),
        turned(eye),
        pad_to(w_out, W, W),
        pad_to(w_up, W, FFH),
        pad_to(w_down, FFH, W),
        gains,
    )


def on_device(
    test_cells,
    train_cells,
    train_present,
    retrieved,
    w_query,
    q_gain,
    w_key,
    k_gain,
    w_value,
    w_out,
    gain_one,
    w_up,
    w_down,
    gain_two,
    cotangent,
):
    owners = lax.axis_size("rows")
    feats = 2
    blocks_own = train_cells.shape[0] // BLK
    wide = train_cells.shape[1]
    wanted = retrieved[0]
    owner_of = wanted // blocks_own
    local_ids = wanted % blocks_own
    places = jnp.arange(owners, dtype=jnp.int32)
    hits = owner_of[None, :] == places[:, None]
    requests = jnp.sum(jnp.where(hits, local_ids[None, :] + 1, 0), axis=1) - 1
    asked = lax.all_to_all(
        requests.reshape(owners, 1), "rows", split_axis=0, concat_axis=0, tiled=True
    ).reshape(-1)
    pick = jnp.clip(asked, 0, blocks_own - 1)
    mask = jnp.repeat(train_present.T != 0, E, axis=1)
    marked = jnp.where(mask, train_cells, jnp.asarray(ABSENT, bf16)).reshape(blocks_own, BLK, wide)
    to_send = pl.pallas_call(
        pick_kernel,
        out_shape=jax.ShapeDtypeStruct((owners, BLK, wide), bf16),
        in_specs=[SMEM_SPEC] + vmem_specs(1),
        out_specs=vmem_specs(1)[0],
        compiler_params=pltpu.CompilerParams(vmem_limit_bytes=LIMIT),
    )(pick, marked)
    rec = lax.all_to_all(to_send, "rows", split_axis=0, concat_axis=0, tiled=True)
    weights = prepare(
        w_query, q_gain, w_key, k_gain, w_value, w_out, gain_one, w_up, w_down, gain_two
    )
    out_cells, grad_test, terms, grads = main_call(
        owner_of, rec, test_cells, cotangent, weights, 256
    )
    back = lax.all_to_all(terms, "rows", split_axis=0, concat_axis=0, tiled=True)
    grad_train = pl.pallas_call(
        sum_kernel,
        out_shape=jax.ShapeDtypeStruct((blocks_own, BLK, wide), bf16),
        in_specs=[SMEM_SPEC] + vmem_specs(1),
        out_specs=vmem_specs(1)[0],
        scratch_shapes=[pltpu.VMEM((blocks_own, BLK, wide), f32)],
        compiler_params=pltpu.CompilerParams(vmem_limit_bytes=LIMIT),
    )(asked, back).reshape(blocks_own * BLK, wide)
    return (out_cells, grad_test, grad_train) + sum_grads(grads)


def small_call(kernel, out_shape, *args):
    return pl.pallas_call(
        kernel,
        out_shape=out_shape,
        in_specs=vmem_specs(len(args)),
        out_specs=jax.tree.map(lambda _: vmem_specs(1)[0], out_shape),
    )(*args)


def sum_grads(grads):
    owners, feats = lax.axis_size("rows"), lax.axis_size("feat")
    share = GRAD_ROWS // feats
    piece = share // owners
    parts = lax.all_to_all(
        grads.reshape(feats, share, 128), "feat", split_axis=0, concat_axis=0, tiled=True
    )
    over_feat = small_call(add_kernel, jax.ShapeDtypeStruct((share, 128), bf16), parts)
    parts = lax.all_to_all(
        over_feat.reshape(owners, piece, 128), "rows", split_axis=0, concat_axis=0, tiled=True
    )
    copies = small_call(
        add_copies_kernel, jax.ShapeDtypeStruct((owners, piece, 128), bf16), parts
    )
    over_all = lax.all_to_all(copies, "rows", split_axis=0, concat_axis=0, tiled=True)
    total = lax.all_gather(over_all.reshape(share, 128), "feat", tiled=True)
    square = jax.ShapeDtypeStruct((E, E), f32)
    return small_call(
        unpack_kernel,
        (square,) * 4
        + (jax.ShapeDtypeStruct((E, FFH), f32), jax.ShapeDtypeStruct((FFH, E), f32)),
        total,
    )


def solution(mesh):
    in_specs = (
        P("rows", "feat"),
        P("rows", "feat"),
        P("feat", "rows"),
        P("rows", None),
        P(),
        P(),
        P(),
        P(),
        P(),
        P(),
        P(),
        P(),
        P(),
        P(),
        P("rows", "feat"),
    )
    out_specs = (
        P("rows", "feat"),
        P("rows", "feat"),
        P("rows", "feat"),
        P(),
        P(),
        P(),
        P(),
        P(),
        P(),
    )
    return jax.shard_map(
        on_device, mesh=mesh, in_specs=in_specs, out_specs=out_specs, check_vma=False
    )
```

```python
import functools
import math

import jax
import jax.numpy as jnp
from jax import lax
from jax.experimental import pallas as pl
from jax.experimental.pallas import tpu as pltpu
from jax.sharding import PartitionSpec as P

H = 6
BLK = 64
E = 192
W = 256
FFH = 768
SIZE = E // H
TEMPER = 1.5 / math.sqrt(SIZE)
LOG2E = math.log2(math.e)
GELU_C = math.sqrt(2.0 / math.pi)
ABSENT = 8.0
ABSENT_ABOVE = 7.0
MASKED = -30000.0
GRAD_ROWS = 4096

bf16 = jnp.bfloat16
f32 = jnp.float32


def dot_nn(a, b):
    return lax.dot_general(a, b, (((1,), (0,)), ((), ())), preferred_element_type=f32)


def dot_nt(a, b):
    return lax.dot_general(a, b, (((1,), (1,)), ((), ())), preferred_element_type=f32)


def dot_tn(a, b):
    return lax.dot_general(a, b, (((0,), (0,)), ((), ())), preferred_element_type=f32)


def pick_kernel(asked_ref, cells_ref, out_ref, sem):
    def body(slot, carry):
        pltpu.make_async_copy(
            cells_ref.at[jnp.maximum(asked_ref[slot], 0)], out_ref.at[slot], sem
        ).start()
        return carry

    lax.fori_loop(0, out_ref.shape[0], body, 0)
    pltpu.make_async_copy(out_ref, out_ref, sem).wait()


def add_terms(asked_ref, back_ref, acc_ref):
    def body(slot, carry):
        asked = asked_ref[slot]

        @pl.when(asked >= 0)
        def _():
            acc_ref[asked] += back_ref[slot, : acc_ref.shape[1]].astype(f32)

        return carry

    lax.fori_loop(0, back_ref.shape[0], body, 0)


def sum_kernel(asked_ref, one_ref, two_ref, acc_ref):
    for part, ref in enumerate((one_ref, two_ref)):
        mine = acc_ref.at[part]
        mine[...] = jnp.zeros(mine.shape, f32)
        add_terms(asked_ref, ref, mine)


def last_kernel(asked_ref, sums_ref, three_ref, out_ref, acc_ref):
    acc_ref[...] = jnp.zeros_like(acc_ref)
    add_terms(asked_ref, three_ref, acc_ref)
    one, two, three = sums_ref[0], sums_ref[1], acc_ref[...]
    out_ref[:, :, 0:128] = jnp.concatenate([one, two[:, :16]], axis=1).astype(bf16)
    out_ref[:, :, 128:256] = jnp.concatenate([two[:, 16:], three[:, :32]], axis=1).astype(bf16)
    out_ref[:, :, 256:384] = three[:, 32:].astype(bf16)


def mean_e(x):
    return jnp.sum(x, axis=-1, keepdims=True) * (1.0 / E)


def head_blocks(full):
    return jnp.concatenate(
        [full[SIZE * h : SIZE * (h + 1), 128 * h : 128 * (h + 1)] for h in range(H)]
        + [jnp.zeros((W - E, 128), f32)],
        axis=0,
    )


def spread_columns(tall, last):
    row = lax.broadcasted_iota(jnp.int32, tall.shape, 0)
    parts = []
    for h in range(H):
        inside = (row >= SIZE * h) & (row < SIZE * (h + 1))
        part = jnp.where(inside, tall, 0.0)
        if last:
            part = jnp.where(row == E, 1.0, part)
        parts.append(part)
    return jnp.concatenate(parts, axis=1).astype(bf16)


def spread_rows(wide):
    lane = lax.broadcasted_iota(jnp.int32, wide.shape, 1)
    parts = []
    for h in range(H):
        inside = (lane >= SIZE * h) & (lane < SIZE * (h + 1))
        parts.append(jnp.where(inside, wide, 0.0))
    return jnp.concatenate(parts, axis=0).astype(bf16)


def layer_norm(x, lane_in):
    centred = jnp.where(lane_in, x - mean_e(x), 0.0)
    scale = lax.rsqrt(mean_e(centred * centred) + 1e-05)
    return centred * scale, scale


def layer_norm_back(hat, scale, gain, dy):
    u = dy * gain
    return scale * (u - mean_e(u) - hat * mean_e(u * hat))


def rms_back(pre, scale, gain, dy):
    u = dy * gain
    return scale * (u - pre * (scale * scale) * mean_e(pre * u))


def widen(x, cols):
    return jnp.concatenate([x, jnp.zeros((x.shape[0], cols - x.shape[1]), x.dtype)], axis=1)


def heighten(x, rows):
    return jnp.concatenate([x, jnp.zeros((rows - x.shape[0], x.shape[1]), x.dtype)], axis=0)


def prepare_kernel(
    test_ref,
    cot_ref,
    w_query_ref,
    w_key_ref,
    w_value_ref,
    w_out_ref,
    w_up_ref,
    w_down_t_ref,
    q_gain_ref,
    k_gain_ref,
    gain_one_ref,
    gain_two_ref,
    projections_ref,
    ffn_ref,
    gains_ref,
    cells_ref,
    q_pre_ref,
    q_tall_ref,
    q_rows_ref,
):
    rows = test_ref.shape[0]
    row = lax.broadcasted_iota(jnp.int32, (E, W), 0)
    lane = lax.broadcasted_iota(jnp.int32, (E, W), 1)
    place = jnp.where(row == lane, 1.0, 0.0).astype(bf16)
    first = jnp.where((row == 0) & (lane == E), 1.0, 0.0).astype(bf16)
    nothing = jnp.zeros((E, W), bf16)
    weights = (
        widen(w_query_ref[...], W),
        widen(w_key_ref[...], W) + first,
        widen(w_value_ref[...], W),
        place,
    )
    for i, weight in enumerate(weights):
        for f in range(2):
            projections_ref[i, f, f * E : (f + 1) * E, :] = weight
            projections_ref[i, f, (1 - f) * E : (2 - f) * E, :] = nothing
    ffn_ref[:, :FFH] = heighten(w_up_ref[...], W)
    ffn_ref[:, FFH : 2 * FFH] = heighten(w_down_t_ref[...], W)
    ffn_ref[:, 2 * FFH :] = heighten(widen(w_out_ref[...], W), W)
    for i, ref in enumerate((q_gain_ref, k_gain_ref, gain_one_ref, gain_two_ref)):
        gains_ref[i : i + 1, :] = widen(ref[...], W)
    test = test_ref[...]
    cot = cot_ref[...]
    q_gain = gains_ref[0:1, :]
    for f in range(2):
        here = slice(f * rows, (f + 1) * rows)
        cells_ref[0, here, :] = dot_nn(test, projections_ref[3, f])
        cells_ref[1, here, :] = dot_nn(cot, projections_ref[3, f])
        pre = dot_nn(test, projections_ref[0, f])
        norm = pre * lax.rsqrt(mean_e(pre * pre) + 1e-06) * q_gain
        norm = norm.astype(bf16).astype(f32)
        q_pre_ref[here, :] = pre
        q_tall_ref[f] = spread_columns(norm.T, True)
        q_rows_ref[f] = spread_rows(norm)


def main_kernel(
    chunk,
    owner_ref,
    rec_hbm,
    projections_hbm,
    ffn_hbm,
    gains_hbm,
    cells_hbm,
    q_pre_hbm,
    q_tall_hbm,
    q_rows_hbm,
    out_ref,
    grad_test_ref,
    one_ref,
    two_ref,
    three_ref,
    grads_ref,
    projections_ref,
    ffn_ref,
    gains_ref,
    cells_ref,
    q_pre_ref,
    q_tall_ref,
    q_rows_ref,
    cells_s,
    kp_s,
    k_s,
    v_s,
    e_s,
    p_s,
    d_s,
    rec_sem,
    sems,
):
    count = owner_ref.shape[0]
    feats = 2
    rows = out_ref.shape[0]
    keys = count * BLK
    chunks = keys // chunk

    def gather(j, carry):
        pltpu.make_async_copy(
            rec_hbm.at[owner_ref[j]],
            cells_s.at[pl.ds(pl.multiple_of(j * BLK, BLK), BLK), :],
            rec_sem,
        ).start()
        return carry

    lax.fori_loop(0, count, gather, 0)
    copies = [
        pltpu.make_async_copy(source, target, sems.at[i])
        for i, (source, target) in enumerate(
            (
                (projections_hbm, projections_ref),
                (gains_hbm, gains_ref),
                (q_tall_hbm, q_tall_ref),
                (ffn_hbm, ffn_ref),
                (cells_hbm, cells_ref),
                (q_pre_hbm, q_pre_ref),
                (q_rows_hbm, q_rows_ref),
            )
        )
    ]
    for copy in copies:
        copy.start()
    one_ref[...] = jnp.zeros_like(one_ref)
    two_ref[...] = jnp.zeros_like(two_ref)
    three_ref[...] = jnp.zeros_like(three_ref)
    pltpu.make_async_copy(cells_s, cells_s, rec_sem).wait()
    for copy in copies:
        copy.wait()

    q_gain = gains_ref[0:1, :]
    k_gain = gains_ref[1:2, :]
    gain_one = gains_ref[2:3, :]
    gain_two = gains_ref[3:4, :]

    def scores(c, totals):
        start = pl.ds(pl.multiple_of(c * chunk, chunk), chunk)
        cells = cells_s[start, :]
        result = []
        for f in range(feats):
            pre = dot_nn(cells, projections_ref[1, f])
            lane = lax.broadcasted_iota(jnp.int32, pre.shape, 1)
            body = jnp.where(lane < E, pre, 0.0)
            scale = lax.rsqrt(mean_e(body * body) + 1e-06)
            norm = body * scale * k_gain
            bias = jnp.where((lane == E) & (pre > ABSENT_ABOVE), MASKED, 0.0)
            norm = (norm + bias).astype(bf16)
            kp_s[f, start, :] = body
            k_s[f, start, :] = norm
            v_s[f, start, :] = dot_nn(cells, projections_ref[2, f]).astype(bf16)
            e = jnp.exp2(dot_nn(norm, q_tall_ref[f]) * (TEMPER * LOG2E))
            e_s[f, start, :] = e
            result.append(totals[f] + jnp.sum(e, axis=0, keepdims=True))
        return tuple(result)

    zero = jnp.zeros((1, H * rows), f32)
    totals = lax.fori_loop(0, chunks, scores, (zero,) * feats)
    inverse = [1.0 / total for total in totals]

    def attend(c, mixed):
        start = pl.ds(pl.multiple_of(c * chunk, chunk), chunk)
        result = []
        for f in range(feats):
            p = (e_s[f, start, :] * inverse[f]).astype(bf16)
            p_s[f, start, :] = p
            result.append(mixed[f] + dot_tn(v_s[f, start, :], p))
        return tuple(result)

    mixed = lax.fori_loop(0, chunks, attend, (jnp.zeros((W, H * rows), f32),) * feats)
    attended_t = [head_blocks(m) for m in mixed]

    attended = jnp.concatenate([a.T for a in attended_t], axis=0).astype(bf16)
    lane_in = lax.broadcasted_iota(jnp.int32, (feats * rows, W), 1) < E
    w_up = ffn_ref[:, :FFH]
    w_down_t = ffn_ref[:, FFH : 2 * FFH]
    w_out = ffn_ref[:, 2 * FFH :]
    inner_one = cells_ref[0] + dot_nn(attended, w_out)
    hat_one, scale_one = layer_norm(inner_one, lane_in)
    normed_one = (hat_one * gain_one).astype(bf16)
    pre = dot_nn(normed_one, w_up)
    tanh = jnp.tanh(GELU_C * (pre + 0.044715 * (pre * pre * pre)))
    hidden = (0.5 * pre * (1.0 + tanh)).astype(bf16)
    slope = 0.5 * (1.0 + tanh) + (0.5 * GELU_C) * pre * (1.0 - tanh * tanh) * (
        1.0 + (3 * 0.044715) * (pre * pre)
    )
    inner_two = normed_one.astype(f32) + dot_nt(hidden, w_down_t)
    hat_two, scale_two = layer_norm(inner_two, lane_in)
    out = (hat_two * gain_two).astype(bf16)
    out_ref[...] = (
        dot_nt(out[:rows], projections_ref[3, 0]) + dot_nt(out[rows:], projections_ref[3, 1])
    ).astype(bf16)
    d_two = layer_norm_back(hat_two, scale_two, gain_two, cells_ref[1])
    d_two = jnp.where(lane_in, d_two, 0.0)
    d_two_b = d_two.astype(bf16)
    d_pre_b = (dot_nn(d_two_b, w_down_t) * slope).astype(bf16)
    d_normed = d_two + dot_nt(d_pre_b, w_up)
    d_one = layer_norm_back(hat_one, scale_one, gain_one, d_normed)
    d_one = jnp.where(lane_in, d_one, 0.0)
    d_one_b = d_one.astype(bf16)
    d_att = dot_nt(d_one_b, w_out).astype(bf16).astype(f32)
    put_grads(grads_ref, 6, dot_tn(attended, d_one_b)[:E])
    put_grads(grads_ref, 8, dot_tn(normed_one, d_pre_b)[:E])
    put_grads(grads_ref, 14, dot_tn(d_two_b, hidden)[:E])

    da_t, da_rows, dots = [], [], []
    for f in range(feats):
        mine = d_att[f * rows : (f + 1) * rows]
        mine_t = mine.T
        da_t.append(spread_columns(mine_t, False))
        da_rows.append(spread_rows(mine))
        product = mine_t * attended_t[f]
        dots.append(
            jnp.concatenate(
                [
                    jnp.sum(product[SIZE * h : SIZE * (h + 1)], axis=0, keepdims=True)
                    for h in range(H)
                ],
                axis=1,
            )
        )

    def back(c, d_queries):
        start = pl.ds(pl.multiple_of(c * chunk, chunk), chunk)
        result = []
        d_cells = jnp.zeros((chunk, feats * E), f32)
        for f in range(feats):
            grad_w = dot_nn(v_s[f, start, :], da_t[f])
            probs = e_s[f, start, :] * inverse[f]
            d_scores = (probs * (grad_w - dots[f]) * TEMPER).astype(bf16)
            result.append(d_queries[f] + dot_tn(k_s[f, start, :], d_scores))
            d_key = dot_nn(d_scores, q_rows_ref[f])
            d_value = dot_nn(p_s[f, start, :], da_rows[f]).astype(bf16)
            body = kp_s[f, start, :]
            scale = lax.rsqrt(mean_e(body * body) + 1e-06)
            d_kpre = rms_back(body, scale, k_gain, d_key).astype(bf16)
            d_s[start, 2 * f * W : (2 * f + 1) * W] = d_kpre
            d_s[start, (2 * f + 1) * W : (2 * f + 2) * W] = d_value
            d_cells = d_cells + dot_nt(d_kpre, projections_ref[1, f])
            d_cells = d_cells + dot_nt(d_value, projections_ref[2, f])
        d_cells = d_cells.astype(bf16)
        for b in range(chunk // BLK):
            owner = owner_ref[c * (chunk // BLK) + b]
            block = d_cells[b * BLK : (b + 1) * BLK]
            one_ref[owner] = block[:48, :128]
            two_ref[owner, :16] = block[48:, :128]
            two_ref[owner, 16:] = block[:32, 128:256]
            three_ref[owner, :32] = block[32:, 128:256]
            three_ref[owner, 32:] = block[:, 256:]
        return tuple(result)

    d_queries = lax.fori_loop(0, chunks, back, (jnp.zeros((W, H * rows), f32),) * feats)

    d_test = jnp.zeros((rows, feats * E), f32)
    g_query = jnp.zeros((W, W), f32)
    placed = []
    for f in range(feats):
        here = slice(f * rows, (f + 1) * rows)
        d_query = head_blocks(d_queries[f]).T
        pre = q_pre_ref[here, :]
        scale = lax.rsqrt(mean_e(pre * pre) + 1e-06)
        d_qpre = rms_back(pre, scale, q_gain, d_query).astype(bf16)
        g_query = g_query + dot_tn(cells_ref[0, here, :].astype(bf16), d_qpre)
        d_test = d_test + dot_nt(d_qpre, projections_ref[0, f])
        placed.append(d_one[here, :E])
    grad_test_ref[...] = (d_test + jnp.concatenate(placed, axis=1)).astype(bf16)
    put_grads(grads_ref, 0, g_query[:E])
    kv = dot_tn(cells_s[...], d_s[...])
    put_grads(grads_ref, 2, kv[:E, : 2 * W] + kv[E:, 2 * W :])
    grads_ref[20 * E :, :] = jnp.zeros((GRAD_ROWS - 20 * E, 128), bf16)


def put_grads(grads_ref, first, value):
    for i in range(value.shape[1] // 128):
        rows = slice((first + i) * E, (first + i + 1) * E)
        grads_ref[rows, :] = value[:, 128 * i : 128 * (i + 1)].astype(bf16)


def take_grads(ref, first, pieces):
    return jnp.concatenate(
        [ref[(first + i) * E : (first + i + 1) * E, :].astype(f32) for i in range(pieces)], axis=1
    )


def ride_kernel(parts_ref, one_ref, out_ref):
    total = jnp.sum(parts_ref[...].astype(f32), axis=0).astype(bf16)
    out_ref[:, : one_ref.shape[1], :] = one_ref[...]
    out_ref[:, one_ref.shape[1] :, :] = total.reshape(
        out_ref.shape[0], out_ref.shape[1] - one_ref.shape[1], 128
    )


def ride_back_kernel(back_ref, two_ref, out_ref):
    cut = two_ref.shape[1]
    total = jnp.sum(back_ref[:, cut:, :].astype(f32), axis=0).astype(bf16)
    out_ref[:, :cut, :] = two_ref[...]
    out_ref[:, cut:, :] = jnp.broadcast_to(total[None], out_ref[:, cut:, :].shape)


def share_kernel(back_ref, three_in, share_ref, three_out, sem):
    pieces = share_ref.shape[1]
    copy = pltpu.make_async_copy(
        back_ref.at[:, pl.ds(back_ref.shape[1] - pieces, pieces), :], share_ref, sem
    )
    copy.start()
    copy.wait()


def unpack_kernel(in_ref, query_ref, key_ref, value_ref, w_out_ref, up_ref, down_t_ref):
    for i, ref in enumerate((query_ref, key_ref, value_ref, w_out_ref)):
        ref[...] = take_grads(in_ref, 2 * i, 2)[:, :E]
    up_ref[...] = take_grads(in_ref, 8, 6)
    down_t_ref[...] = take_grads(in_ref, 14, 6)


def vmem_specs(n):
    return [pl.BlockSpec(memory_space=pltpu.VMEM)] * n


SMEM_SPEC = pl.BlockSpec(memory_space=pltpu.SMEM)
LIMIT = 48 * 1024 * 1024


ANY_SPEC = pl.BlockSpec(memory_space=pl.ANY)
PARAMS = pltpu.CompilerParams(vmem_limit_bytes=LIMIT)


def shape(dims, dtype=bf16):
    return jax.ShapeDtypeStruct(dims, dtype)


def small_call(kernel, out_shape, *args):
    return pl.pallas_call(
        kernel,
        out_shape=out_shape,
        in_specs=vmem_specs(len(args)),
        out_specs=jax.tree.map(lambda _: vmem_specs(1)[0], out_shape),
        compiler_params=PARAMS,
    )(*args)


def prepare(test_cells, cotangent, weights):
    w_query, q_gain, w_key, k_gain, w_value, w_out, gain_one, w_up, w_down, gain_two = weights
    rows, wide = test_cells.shape
    ht = H * rows
    return small_call(
        prepare_kernel,
        (
            shape((4, 2, wide, W)),
            shape((W, 2 * FFH + W)),
            shape((4, W), f32),
            shape((2, 2 * rows, W), f32),
            shape((2 * rows, W), f32),
            shape((2, W, ht)),
            shape((2, ht, W)),
        ),
        test_cells,
        cotangent,
        w_query,
        w_key,
        w_value,
        w_out,
        w_up,
        w_down.T,
        *(gain.reshape(1, E) for gain in (q_gain, k_gain, gain_one, gain_two)),
    )


def main_call(owner_of, rec, prepared, rows, chunk):
    count = owner_of.shape[0]
    keys = count * BLK
    owners, _, wide = rec.shape
    ht = H * rows
    return pl.pallas_call(
        functools.partial(main_kernel, chunk),
        out_shape=(
            shape((rows, wide)),
            shape((rows, wide)),
            shape((owners, 48, 128)),
            shape((owners, 48, 128)),
            shape((owners, 96, 128)),
            shape((GRAD_ROWS, 128)),
        ),
        in_specs=[SMEM_SPEC] + [ANY_SPEC] * (1 + len(prepared)),
        out_specs=tuple(vmem_specs(6)),
        scratch_shapes=[pltpu.VMEM(x.shape, x.dtype) for x in prepared]
        + [
            pltpu.VMEM((keys, wide), bf16),
            pltpu.VMEM((2, keys, W), f32),
            pltpu.VMEM((2, keys, W), bf16),
            pltpu.VMEM((2, keys, W), bf16),
            pltpu.VMEM((2, keys, ht), f32),
            pltpu.VMEM((2, keys, ht), bf16),
            pltpu.VMEM((keys, 4 * W), bf16),
            pltpu.SemaphoreType.DMA,
            pltpu.SemaphoreType.DMA((len(prepared),)),
        ],
        compiler_params=PARAMS,
    )(owner_of, rec, *prepared)


def swap(x, axis):
    return lax.all_to_all(x, axis, split_axis=0, concat_axis=0, tiled=True)


def unpack_shapes():
    return (shape((E, E), f32),) * 4 + (shape((E, FFH), f32),) * 2


def on_device(
    test_cells,
    train_cells,
    train_present,
    retrieved,
    w_query,
    q_gain,
    w_key,
    k_gain,
    w_value,
    w_out,
    gain_one,
    w_up,
    w_down,
    gain_two,
    cotangent,
):
    owners, groups = lax.axis_size("rows"), lax.axis_size("feat")
    blocks_own = train_cells.shape[0] // BLK
    rows, wide = test_cells.shape
    count = retrieved.shape[1]
    owner_of = retrieved[0] // blocks_own
    table = swap(jnp.broadcast_to(retrieved, (owners, count)).reshape(owners, 1, count), "rows")
    table = table.reshape(owners, count)
    mine = table // blocks_own == lax.axis_index("rows")
    asked = jnp.sum(jnp.where(mine, table % blocks_own + 1, 0), axis=1) - 1
    mask = jnp.repeat(train_present.T != 0, E, axis=1)
    marked = jnp.where(mask, train_cells, jnp.asarray(ABSENT, bf16)).reshape(blocks_own, BLK, wide)
    to_send = pl.pallas_call(
        pick_kernel,
        out_shape=shape((owners, BLK, wide)),
        in_specs=[SMEM_SPEC] + vmem_specs(1),
        out_specs=ANY_SPEC,
        scratch_shapes=[pltpu.SemaphoreType.DMA],
        compiler_params=PARAMS,
    )(asked, marked)
    rec = swap(to_send, "rows")
    prepared = prepare(
        test_cells,
        cotangent,
        (w_query, q_gain, w_key, k_gain, w_value, w_out, gain_one, w_up, w_down, gain_two),
    )
    out_cells, grad_test, one, two, three, grads = main_call(owner_of, rec, prepared, rows, 256)

    share = GRAD_ROWS // groups
    piece = share // owners
    parts = swap(grads.reshape(groups, share, 128), "feat")
    riding = shape((owners, one.shape[1] + piece, 128))
    back_one = swap(small_call(ride_kernel, riding, parts, one), "rows")
    back_two = swap(small_call(ride_back_kernel, riding, back_one, two), "rows")
    over_all, three = pl.pallas_call(
        share_kernel,
        out_shape=(shape((owners, piece, 128)), shape(three.shape)),
        in_specs=[ANY_SPEC] * 2,
        out_specs=(ANY_SPEC,) * 2,
        scratch_shapes=[pltpu.SemaphoreType.DMA],
        input_output_aliases={1: 1},
        compiler_params=PARAMS,
    )(back_two, three)
    total = lax.all_gather(over_all.reshape(share, 128), "feat", tiled=True)
    back_three = swap(three, "rows")
    sums = pl.pallas_call(
        sum_kernel,
        out_shape=shape((2, blocks_own, one.shape[1], 128), f32),
        in_specs=[SMEM_SPEC] + vmem_specs(2),
        out_specs=vmem_specs(1)[0],
        compiler_params=PARAMS,
    )(asked, back_one, back_two)
    grad_train = pl.pallas_call(
        last_kernel,
        out_shape=shape((blocks_own, BLK, wide)),
        in_specs=[SMEM_SPEC] + vmem_specs(2),
        out_specs=vmem_specs(1)[0],
        scratch_shapes=[pltpu.VMEM((blocks_own, three.shape[1], 128), f32)],
        compiler_params=PARAMS,
    )(asked, sums, back_three).reshape(blocks_own * BLK, wide)
    *others, g_down_t = small_call(unpack_kernel, unpack_shapes(), total)
    return (out_cells, grad_test, grad_train, *others, g_down_t.T)


def solution(mesh):
    in_specs = (
        P("rows", "feat"),
        P("rows", "feat"),
        P("feat", "rows"),
        P("rows", None),
        P(),
        P(),
        P(),
        P(),
        P(),
        P(),
        P(),
        P(),
        P(),
        P(),
        P("rows", "feat"),
    )
    out_specs = (
        P("rows", "feat"),
        P("rows", "feat"),
        P("rows", "feat"),
        P(),
        P(),
        P(),
        P(),
        P(),
        P(),
    )
    return jax.shard_map(
        on_device, mesh=mesh, in_specs=in_specs, out_specs=out_specs, check_vma=False
    )
```

```python
import functools
import math

import jax
import jax.numpy as jnp
from jax import lax
from jax.experimental import pallas as pl
from jax.experimental.pallas import tpu as pltpu
from jax.sharding import PartitionSpec as P

H = 6
BLK = 64
E = 192
W = 256
FFH = 768
SIZE = E // H
TEMPER = 1.5 / math.sqrt(SIZE)
LOG2E = math.log2(math.e)
GELU_C = math.sqrt(2.0 / math.pi)
ABSENT = 8.0
ABSENT_ABOVE = 7.0
MASKED = -30000.0
GRAD_ROWS = 4096

bf16 = jnp.bfloat16
f32 = jnp.float32


def dot_nn(a, b):
    return lax.dot_general(a, b, (((1,), (0,)), ((), ())), preferred_element_type=f32)


def dot_nt(a, b):
    return lax.dot_general(a, b, (((1,), (1,)), ((), ())), preferred_element_type=f32)


def dot_tn(a, b):
    return lax.dot_general(a, b, (((0,), (0,)), ((), ())), preferred_element_type=f32)


def pick_kernel(asked_ref, cells_ref, out_ref, sem):
    def body(slot, carry):
        pltpu.make_async_copy(
            cells_ref.at[jnp.maximum(asked_ref[slot], 0)], out_ref.at[slot], sem
        ).start()
        return carry

    lax.fori_loop(0, out_ref.shape[0], body, 0)
    pltpu.make_async_copy(out_ref, out_ref, sem).wait()


def add_terms(asked_ref, back_ref, acc_ref):
    def body(slot, carry):
        asked = asked_ref[slot]

        @pl.when(asked >= 0)
        def _():
            acc_ref[asked] += back_ref[slot, : acc_ref.shape[1]].astype(f32)

        return carry

    lax.fori_loop(0, back_ref.shape[0], body, 0)


def sum_kernel(asked_ref, zero_ref, one_ref, zero_acc, one_acc):
    for ref, acc in ((zero_ref, zero_acc), (one_ref, one_acc)):
        acc[...] = jnp.zeros(acc.shape, f32)
        add_terms(asked_ref, ref, acc)


def last_kernel(asked_ref, zero_ref, one_ref, back_ref, out_ref, acc_ref):
    acc_ref[...] = jnp.zeros_like(acc_ref)
    add_terms(asked_ref, back_ref, acc_ref)
    zero, one, two = zero_ref[...], one_ref[...], acc_ref[...]
    out_ref[:, :, 0:128] = zero[:, :BLK].astype(bf16)
    out_ref[:, :, 128:256] = jnp.concatenate([zero[:, BLK:], one[:, :32]], axis=1).astype(bf16)
    out_ref[:, :, 256:384] = jnp.concatenate([one[:, 32:], two], axis=1).astype(bf16)


def mean_e(x):
    return jnp.sum(x, axis=-1, keepdims=True) * (1.0 / E)


def head_blocks(full):
    return jnp.concatenate(
        [full[SIZE * h : SIZE * (h + 1), 128 * h : 128 * (h + 1)] for h in range(H)]
        + [jnp.zeros((W - E, 128), f32)],
        axis=0,
    )


def spread_columns(tall, last):
    row = lax.broadcasted_iota(jnp.int32, tall.shape, 0)
    parts = []
    for h in range(H):
        inside = (row >= SIZE * h) & (row < SIZE * (h + 1))
        part = jnp.where(inside, tall, 0.0)
        if last:
            part = jnp.where(row == E, 1.0, part)
        parts.append(part)
    return jnp.concatenate(parts, axis=1).astype(bf16)


def spread_rows(wide):
    lane = lax.broadcasted_iota(jnp.int32, wide.shape, 1)
    parts = []
    for h in range(H):
        inside = (lane >= SIZE * h) & (lane < SIZE * (h + 1))
        parts.append(jnp.where(inside, wide, 0.0))
    return jnp.concatenate(parts, axis=0).astype(bf16)


def layer_norm(x, lane_in):
    centred = jnp.where(lane_in, x - mean_e(x), 0.0)
    scale = lax.rsqrt(mean_e(centred * centred) + 1e-05)
    return centred * scale, scale


def layer_norm_back(hat, scale, gain, dy):
    u = dy * gain
    return scale * (u - mean_e(u) - hat * mean_e(u * hat))


def rms_back(pre, scale, gain, dy):
    u = dy * gain
    return scale * (u - pre * (scale * scale) * mean_e(pre * u))


def feature_lanes(f):
    return slice(128 * f, 128 * f + W)


def side_by_side(first, second):
    return jnp.concatenate(
        [first[:, :128], first[:, 128:] + second[:, :128], second[:, 128:]], axis=1
    )


def widen(x, cols):
    return jnp.concatenate([x, jnp.zeros((x.shape[0], cols - x.shape[1]), x.dtype)], axis=1)


def heighten(x, rows):
    return jnp.concatenate([x, jnp.zeros((rows - x.shape[0], x.shape[1]), x.dtype)], axis=0)


def prepare_kernel(
    test_ref,
    cot_ref,
    w_query_ref,
    w_key_ref,
    w_value_ref,
    w_out_ref,
    w_up_ref,
    w_down_t_ref,
    q_gain_ref,
    k_gain_ref,
    gain_one_ref,
    gain_two_ref,
    projections_ref,
    ffn_ref,
    gains_ref,
    cells_ref,
    q_pre_ref,
    q_tall_ref,
    q_rows_ref,
):
    rows = test_ref.shape[0]
    row = lax.broadcasted_iota(jnp.int32, (E, W), 0)
    lane = lax.broadcasted_iota(jnp.int32, (E, W), 1)
    place = jnp.where(row == lane, 1.0, 0.0).astype(bf16)
    first = jnp.where((row == 0) & (lane == E), 1.0, 0.0).astype(bf16)
    nothing = jnp.zeros((W - E, W), bf16)
    weights = (
        widen(w_query_ref[...], W),
        widen(w_key_ref[...], W) + first,
        widen(w_value_ref[...], W),
        place,
    )
    for i, weight in enumerate(weights):
        for f in range(2):
            skip = f * (W - E)
            projections_ref[i, f, skip : skip + E, :] = weight
            projections_ref[i, f, (1 - f) * E : (1 - f) * E + W - E, :] = nothing
    ffn_ref[:, :FFH] = heighten(w_up_ref[...], W)
    ffn_ref[:, FFH : 2 * FFH] = heighten(w_down_t_ref[...], W)
    ffn_ref[:, 2 * FFH :] = heighten(widen(w_out_ref[...], W), W)
    for i, ref in enumerate((q_gain_ref, k_gain_ref, gain_one_ref, gain_two_ref)):
        gains_ref[i : i + 1, :] = widen(ref[...], W)
    test = test_ref[...]
    cot = cot_ref[...]
    q_gain = gains_ref[0:1, :]
    for f in range(2):
        here = slice(f * rows, (f + 1) * rows)
        lanes = feature_lanes(f)
        cells_ref[0, here, :] = dot_nn(test[:, lanes], projections_ref[3, f])
        cells_ref[1, here, :] = dot_nn(cot[:, lanes], projections_ref[3, f])
        pre = dot_nn(test[:, lanes], projections_ref[0, f])
        norm = pre * lax.rsqrt(mean_e(pre * pre) + 1e-06) * q_gain
        norm = norm.astype(bf16).astype(f32)
        q_pre_ref[here, :] = pre
        q_tall_ref[f] = spread_columns(norm.T, True)
        q_rows_ref[f] = spread_rows(norm)


def main_kernel(
    chunk,
    owner_ref,
    core_ref,
    rec_hbm,
    projections_hbm,
    ffn_hbm,
    gains_hbm,
    cells_hbm,
    q_pre_hbm,
    q_tall_hbm,
    q_rows_hbm,
    out_ref,
    grad_test_ref,
    zero_ref,
    one_ref,
    two_ref,
    keep_hbm,
    give_hbm,
    projections_ref,
    ffn_ref,
    gains_ref,
    cells_ref,
    q_pre_ref,
    q_tall_ref,
    q_rows_ref,
    cells_s,
    kp_s,
    k_s,
    v_s,
    e_s,
    p_s,
    d_s,
    grads_ref,
    rec_sem,
    sems,
):
    count = owner_ref.shape[0]
    feats = 2
    rows = out_ref.shape[0]
    keys = count * BLK
    chunks = keys // chunk

    def gather(j, carry):
        pltpu.make_async_copy(
            rec_hbm.at[owner_ref[j]],
            cells_s.at[pl.ds(pl.multiple_of(j * BLK, BLK), BLK), :],
            rec_sem,
        ).start()
        return carry

    lax.fori_loop(0, count, gather, 0)
    copies = [
        pltpu.make_async_copy(source, target, sems.at[i])
        for i, (source, target) in enumerate(
            (
                (projections_hbm, projections_ref),
                (gains_hbm, gains_ref),
                (q_tall_hbm, q_tall_ref),
                (ffn_hbm, ffn_ref),
                (cells_hbm, cells_ref),
                (q_pre_hbm, q_pre_ref),
                (q_rows_hbm, q_rows_ref),
            )
        )
    ]
    for copy in copies:
        copy.start()
    zero_ref[...] = jnp.zeros_like(zero_ref)
    one_ref[...] = jnp.zeros_like(one_ref)
    two_ref[...] = jnp.zeros_like(two_ref)
    pltpu.make_async_copy(cells_s, cells_s, rec_sem).wait()
    for copy in copies:
        copy.wait()

    q_gain = gains_ref[0:1, :]
    k_gain = gains_ref[1:2, :]
    gain_one = gains_ref[2:3, :]
    gain_two = gains_ref[3:4, :]

    def scores(c, totals):
        start = pl.ds(pl.multiple_of(c * chunk, chunk), chunk)
        result = []
        for f in range(feats):
            pre = dot_nn(cells_s[start, feature_lanes(f)], projections_ref[1, f])
            lane = lax.broadcasted_iota(jnp.int32, pre.shape, 1)
            body = jnp.where(lane < E, pre, 0.0)
            scale = lax.rsqrt(mean_e(body * body) + 1e-06)
            norm = body * scale * k_gain
            bias = jnp.where((lane == E) & (pre > ABSENT_ABOVE), MASKED, 0.0)
            norm = (norm + bias).astype(bf16)
            kp_s[f, start, :] = body
            k_s[f, start, :] = norm
            v_s[f, start, :] = dot_nn(cells_s[start, feature_lanes(f)], projections_ref[2, f]).astype(bf16)
            e = jnp.exp2(dot_nn(norm, q_tall_ref[f]) * (TEMPER * LOG2E))
            e_s[f, start, :] = e
            result.append(totals[f] + jnp.sum(e, axis=0, keepdims=True))
        return tuple(result)

    zero = jnp.zeros((1, H * rows), f32)
    totals = lax.fori_loop(0, chunks, scores, (zero,) * feats)
    inverse = [1.0 / total for total in totals]
    inverse_tempered = [TEMPER / total for total in totals]

    def attend(c, mixed):
        start = pl.ds(pl.multiple_of(c * chunk, chunk), chunk)
        result = []
        for f in range(feats):
            p = (e_s[f, start, :] * inverse[f]).astype(bf16)
            p_s[f, start, :] = p
            result.append(mixed[f] + dot_tn(v_s[f, start, :E], p))
        return tuple(result)

    mixed = lax.fori_loop(0, chunks, attend, (jnp.zeros((E, H * rows), f32),) * feats)
    attended_t = [head_blocks(m) for m in mixed]

    attended = jnp.concatenate([a.T for a in attended_t], axis=0).astype(bf16)
    lane_in = lax.broadcasted_iota(jnp.int32, (feats * rows, W), 1) < E
    w_up = ffn_ref[:, :FFH]
    w_down_t = ffn_ref[:, FFH : 2 * FFH]
    w_out = ffn_ref[:, 2 * FFH :]
    inner_one = cells_ref[0] + dot_nn(attended, w_out)
    hat_one, scale_one = layer_norm(inner_one, lane_in)
    normed_one = (hat_one * gain_one).astype(bf16)
    pre = dot_nn(normed_one, w_up)
    tanh = jnp.tanh(GELU_C * (pre + 0.044715 * (pre * pre * pre)))
    hidden = (0.5 * pre * (1.0 + tanh)).astype(bf16)
    slope = 0.5 * (1.0 + tanh) + (0.5 * GELU_C) * pre * (1.0 - tanh * tanh) * (
        1.0 + (3 * 0.044715) * (pre * pre)
    )
    inner_two = normed_one.astype(f32) + dot_nt(hidden, w_down_t)
    hat_two, scale_two = layer_norm(inner_two, lane_in)
    out = (hat_two * gain_two).astype(bf16)
    out_ref[...] = side_by_side(
        dot_nt(out[:rows], projections_ref[3, 0]), dot_nt(out[rows:], projections_ref[3, 1])
    ).astype(bf16)
    d_two = layer_norm_back(hat_two, scale_two, gain_two, cells_ref[1])
    d_two = jnp.where(lane_in, d_two, 0.0)
    d_two_b = d_two.astype(bf16)
    d_pre_b = (dot_nn(d_two_b, w_down_t) * slope).astype(bf16)
    d_normed = d_two + dot_nt(d_pre_b, w_up)
    d_one = layer_norm_back(hat_one, scale_one, gain_one, d_normed)
    d_one = jnp.where(lane_in, d_one, 0.0)
    d_one_b = d_one.astype(bf16)
    d_att = dot_nt(d_one_b, w_out).astype(bf16).astype(f32)
    put_grads(grads_ref, 6, dot_tn(attended, d_one_b)[:E])
    put_grads(grads_ref, 8, dot_tn(normed_one, d_pre_b)[:E])
    put_grads(grads_ref, 14, dot_tn(d_two_b, hidden)[:E])

    da_t, da_rows, dots = [], [], []
    for f in range(feats):
        mine = d_att[f * rows : (f + 1) * rows]
        mine_t = mine.T
        da_t.append(spread_columns(mine_t, False))
        da_rows.append(spread_rows(mine))
        product = mine_t * attended_t[f]
        dots.append(
            jnp.concatenate(
                [
                    jnp.sum(product[SIZE * h : SIZE * (h + 1)], axis=0, keepdims=True)
                    for h in range(H)
                ],
                axis=1,
            )
        )

    def back(c, d_queries):
        start = pl.ds(pl.multiple_of(c * chunk, chunk), chunk)
        result = []
        d_cells = []
        for f in range(feats):
            grad_w = dot_nn(v_s[f, start, :], da_t[f])
            probs = e_s[f, start, :] * inverse_tempered[f]
            d_scores = (probs * (grad_w - dots[f])).astype(bf16)
            result.append(d_queries[f] + dot_tn(k_s[f, start, :E], d_scores))
            d_key = dot_nn(d_scores, q_rows_ref[f])
            d_value = dot_nn(p_s[f, start, :], da_rows[f]).astype(bf16)
            body = kp_s[f, start, :]
            scale = lax.rsqrt(mean_e(body * body) + 1e-06)
            d_kpre = rms_back(body, scale, k_gain, d_key).astype(bf16)
            d_s[start, 2 * f * W : (2 * f + 1) * W] = d_kpre
            d_s[start, (2 * f + 1) * W : (2 * f + 2) * W] = d_value
            d_cells.append(
                dot_nt(d_kpre, projections_ref[1, f]) + dot_nt(d_value, projections_ref[2, f])
            )
        d_cells = side_by_side(*d_cells).astype(bf16)
        for b in range(chunk // BLK):
            owner = owner_ref[c * (chunk // BLK) + b]
            block = d_cells[b * BLK : (b + 1) * BLK]
            zero_ref[owner, :BLK] = block[:, :128]
            zero_ref[owner, BLK:] = block[:32, 128:256]
            one_ref[owner, :32] = block[32:, 128:256]
            one_ref[owner, 32:] = block[:16, 256:]
            two_ref[owner] = block[16:, 256:]
        return tuple(result)

    d_queries = lax.fori_loop(0, chunks, back, (jnp.zeros((E, H * rows), f32),) * feats)

    d_test = []
    g_query = jnp.zeros((W, W), f32)
    placed = []
    for f in range(feats):
        here = slice(f * rows, (f + 1) * rows)
        d_query = head_blocks(d_queries[f]).T
        pre = q_pre_ref[here, :]
        scale = lax.rsqrt(mean_e(pre * pre) + 1e-06)
        d_qpre = rms_back(pre, scale, q_gain, d_query).astype(bf16)
        g_query = g_query + dot_tn(cells_ref[0, here, :].astype(bf16), d_qpre)
        d_test.append(dot_nt(d_qpre, projections_ref[0, f]))
        placed.append(d_one[here, :E])
    grad_test_ref[...] = (side_by_side(*d_test) + jnp.concatenate(placed, axis=1)).astype(bf16)
    put_grads(grads_ref, 0, g_query[:E])
    kv = jnp.zeros((E, 2 * W), f32)
    for f in range(feats):
        both = dot_tn(cells_s[:, feature_lanes(f)], d_s[:, 2 * f * W : 2 * (f + 1) * W])
        kv = kv + both[f * (W - E) : f * (W - E) + E]
    put_grads(grads_ref, 2, kv)
    grads_ref[20 * E :, :] = jnp.zeros((GRAD_ROWS - 20 * E, 128), bf16)
    core = core_ref[0]
    halves = [
        pltpu.make_async_copy(
            grads_ref.at[pl.ds(pl.multiple_of(half * (GRAD_ROWS // 2), 128), GRAD_ROWS // 2), :],
            target,
            sems.at[i],
        )
        for i, (half, target) in enumerate(((core, keep_hbm), (1 - core, give_hbm)))
    ]
    for copy in halves:
        copy.start()
    for copy in halves:
        copy.wait()


def put_grads(grads_ref, first, value):
    for i in range(value.shape[1] // 128):
        rows = slice((first + i) * E, (first + i + 1) * E)
        grads_ref[rows, :] = value[:, 128 * i : 128 * (i + 1)].astype(bf16)


def take_grads(ref, first, pieces):
    return jnp.concatenate(
        [ref[(first + i) * E : (first + i + 1) * E, :].astype(f32) for i in range(pieces)], axis=1
    )


def halve_kernel(bit_ref, keep_ref, got_ref, next_keep_ref, next_give_ref):
    half = next_keep_ref.shape[0]
    bit = bit_ref[0]
    for part, ref in ((bit, next_keep_ref), (1 - bit, next_give_ref)):
        rows = pl.ds(pl.multiple_of(part * half, 128), half)
        ref[...] = (keep_ref[rows, :].astype(f32) + got_ref[rows, :].astype(f32)).astype(bf16)


def ride_kernel(keep_ref, got_ref, one_ref, out_ref):
    cut = one_ref.shape[1]
    total = (keep_ref[...].astype(f32) + got_ref[...].astype(f32)).astype(bf16)
    out_ref[:, :cut, :] = one_ref[...]
    out_ref[:, cut:, :] = total.reshape(out_ref.shape[0], out_ref.shape[1] - cut, 128)


def ride_back_kernel(back_ref, two_ref, out_ref):
    cut = two_ref.shape[1]
    total = jnp.sum(back_ref[:, cut:, :].astype(f32), axis=0).astype(bf16)
    out_ref[:, :cut, :] = two_ref[...]
    out_ref[:, cut:, :] = jnp.broadcast_to(total[None], out_ref[:, cut:, :].shape)


def share_kernel(back_ref, out_ref):
    pieces = out_ref.shape[1] // back_ref.shape[0]
    share = back_ref[:, back_ref.shape[1] - pieces :, :].reshape(out_ref.shape[1], 128)
    out_ref[...] = jnp.broadcast_to(share[None], out_ref.shape)


def unpack_kernel(
    core_ref, mine_ref, got_ref, query_ref, key_ref, value_ref, w_out_ref, up_ref, down_t_ref, all_ref
):
    chips, share, _ = mine_ref.shape
    core = core_ref[0]
    for half, ref in ((core, mine_ref), (1 - core, got_ref)):
        for chip in range(chips):
            place = (chip % 2) * 2 + chip // 2
            start = pl.multiple_of(half * (chips * share) + place * share, 128)
            all_ref[pl.ds(start, share), :] = ref[chip]
    for i, ref in enumerate((query_ref, key_ref, value_ref, w_out_ref)):
        ref[...] = take_grads(all_ref, 2 * i, 2)[:, :E]
    up_ref[...] = take_grads(all_ref, 8, 6)
    down_t_ref[...] = take_grads(all_ref, 14, 6)


def vmem_specs(n):
    return [pl.BlockSpec(memory_space=pltpu.VMEM)] * n


SMEM_SPEC = pl.BlockSpec(memory_space=pltpu.SMEM)
LIMIT = 48 * 1024 * 1024


ANY_SPEC = pl.BlockSpec(memory_space=pl.ANY)
PARAMS = pltpu.CompilerParams(vmem_limit_bytes=LIMIT)


def shape(dims, dtype=bf16):
    return jax.ShapeDtypeStruct(dims, dtype)


def small_call(kernel, out_shape, *args, scalars=(), scratch=()):
    return pl.pallas_call(
        kernel,
        out_shape=out_shape,
        in_specs=[SMEM_SPEC] * len(scalars) + vmem_specs(len(args)),
        out_specs=jax.tree.map(lambda _: vmem_specs(1)[0], out_shape),
        scratch_shapes=scratch,
        compiler_params=PARAMS,
    )(*scalars, *args)


def prepare(test_cells, cotangent, weights):
    w_query, q_gain, w_key, k_gain, w_value, w_out, gain_one, w_up, w_down, gain_two = weights
    rows, wide = test_cells.shape
    ht = H * rows
    return small_call(
        prepare_kernel,
        (
            shape((4, 2, W, W)),
            shape((W, 2 * FFH + W)),
            shape((4, W), f32),
            shape((2, 2 * rows, W), f32),
            shape((2 * rows, W), f32),
            shape((2, W, ht)),
            shape((2, ht, W)),
        ),
        test_cells,
        cotangent,
        w_query,
        w_key,
        w_value,
        w_out,
        w_up,
        w_down.T,
        *(gain.reshape(1, E) for gain in (q_gain, k_gain, gain_one, gain_two)),
    )


def main_call(owner_of, core, rec, prepared, rows, chunk):
    count = owner_of.shape[0]
    keys = count * BLK
    owners, _, wide = rec.shape
    ht = H * rows
    return pl.pallas_call(
        functools.partial(main_kernel, chunk),
        out_shape=(
            shape((rows, wide)),
            shape((rows, wide)),
            shape((owners, 96, 128)),
            shape((owners, 48, 128)),
            shape((owners, 48, 128)),
            shape((GRAD_ROWS // 2, 128)),
            shape((GRAD_ROWS // 2, 128)),
        ),
        in_specs=[SMEM_SPEC] * 2 + [ANY_SPEC] * (1 + len(prepared)),
        out_specs=tuple(vmem_specs(5)) + (ANY_SPEC,) * 2,
        scratch_shapes=[pltpu.VMEM(x.shape, x.dtype) for x in prepared]
        + [
            pltpu.VMEM((keys, wide), bf16),
            pltpu.VMEM((2, keys, W), f32),
            pltpu.VMEM((2, keys, W), bf16),
            pltpu.VMEM((2, keys, W), bf16),
            pltpu.VMEM((2, keys, ht), f32),
            pltpu.VMEM((2, keys, ht), bf16),
            pltpu.VMEM((keys, 4 * W), bf16),
            pltpu.VMEM((GRAD_ROWS, 128), bf16),
            pltpu.SemaphoreType.DMA,
            pltpu.SemaphoreType.DMA((len(prepared),)),
        ],
        compiler_params=PARAMS,
    )(owner_of, core, rec, *prepared)


def swap(x, axis):
    return lax.all_to_all(x, axis, split_axis=0, concat_axis=0, tiled=True)


def on_device(
    test_cells,
    train_cells,
    train_present,
    retrieved,
    w_query,
    q_gain,
    w_key,
    k_gain,
    w_value,
    w_out,
    gain_one,
    w_up,
    w_down,
    gain_two,
    cotangent,
):
    owners, groups = lax.axis_size("rows"), lax.axis_size("feat")
    blocks_own = train_cells.shape[0] // BLK
    rows, wide = test_cells.shape
    count = retrieved.shape[1]
    owner_of = retrieved[0] // blocks_own
    table = swap(jnp.broadcast_to(retrieved, (owners, count)).reshape(owners, 1, count), "rows")
    table = table.reshape(owners, count)
    mine = table // blocks_own == lax.axis_index("rows")
    asked = jnp.sum(jnp.where(mine, table % blocks_own + 1, 0), axis=1) - 1
    mask = jnp.repeat(train_present.T != 0, E, axis=1)
    marked = jnp.where(mask, train_cells, jnp.asarray(ABSENT, bf16)).reshape(blocks_own, BLK, wide)
    to_send = pl.pallas_call(
        pick_kernel,
        out_shape=shape((owners, BLK, wide)),
        in_specs=[SMEM_SPEC] + vmem_specs(1),
        out_specs=ANY_SPEC,
        scratch_shapes=[pltpu.SemaphoreType.DMA],
        compiler_params=PARAMS,
    )(asked, marked)
    rec = swap(to_send, "rows")
    prepared = prepare(
        test_cells,
        cotangent,
        (w_query, q_gain, w_key, k_gain, w_value, w_out, gain_one, w_up, w_down, gain_two),
    )
    feat = lax.axis_index("feat")
    core, low, high = ((feat // bit % 2).reshape(1) for bit in (1, 2, 4))
    out_cells, grad_test, zero, one, two, keep, give = main_call(
        owner_of, core, rec, prepared, rows, 1024
    )

    back_zero = swap(zero, "rows")
    got = flip(give, 1)
    half = keep.shape[0] // 2
    keep, give = small_call(halve_kernel, (shape((half, 128)),) * 2, keep, got, scalars=(low,))
    got = flip(give, 2)
    half = half // 2
    keep, give = small_call(halve_kernel, (shape((half, 128)),) * 2, keep, got, scalars=(high,))
    got = flip(give, 4)
    piece = half // owners
    riding = shape((owners, one.shape[1] + piece, 128))
    back_one = swap(small_call(ride_kernel, riding, keep, got, one), "rows")
    back_two = swap(small_call(ride_back_kernel, riding, back_one, two), "rows")
    chips = groups // 2
    copies = small_call(share_kernel, shape((chips, half, 128)), back_two)
    mine = lax.all_to_all(
        copies,
        "feat",
        split_axis=0,
        concat_axis=0,
        tiled=True,
        axis_index_groups=[[2 * chip + c for chip in range(chips)] for c in range(2)],
    )
    others = flip(mine, 1)
    sums = small_call(
        sum_kernel,
        tuple(shape((blocks_own, x.shape[1], 128), f32) for x in (zero, one)),
        back_zero,
        back_one,
        scalars=(asked,),
    )
    grad_train = small_call(
        last_kernel,
        shape((blocks_own, BLK, wide)),
        *sums,
        back_two,
        scalars=(asked,),
        scratch=[pltpu.VMEM((blocks_own, two.shape[1], 128), f32)],
    ).reshape(blocks_own * BLK, wide)
    *weights, g_down_t = unpack(core, mine, others)
    return (out_cells, grad_test, grad_train, *weights, g_down_t.T)


def flip(x, bit):
    count = lax.axis_size("feat")
    return lax.ppermute(x, "feat", [(i, i ^ bit) for i in range(count)])


def unpack(core, mine, others):
    return small_call(
        unpack_kernel,
        (shape((E, E), f32),) * 4 + (shape((E, FFH), f32),) * 2,
        mine,
        others,
        scalars=(core,),
        scratch=[pltpu.VMEM((GRAD_ROWS, 128), bf16)],
    )


def solution(mesh):
    in_specs = (
        P("rows", "feat"),
        P("rows", "feat"),
        P("feat", "rows"),
        P("rows", None),
        P(),
        P(),
        P(),
        P(),
        P(),
        P(),
        P(),
        P(),
        P(),
        P(),
        P("rows", "feat"),
    )
    out_specs = (
        P("rows", "feat"),
        P("rows", "feat"),
        P("rows", "feat"),
        P(),
        P(),
        P(),
        P(),
        P(),
        P(),
    )
    return jax.shard_map(
        on_device, mesh=mesh, in_specs=in_specs, out_specs=out_specs, check_vma=False
    )
```

```python
import functools
import math

import jax
import jax.numpy as jnp
from jax import lax
from jax.experimental import pallas as pl
from jax.experimental.pallas import tpu as pltpu
from jax.sharding import PartitionSpec as P

H = 6
BLK = 64
E = 192
W = 256
FFH = 768
SIZE = E // H
TEMPER = 1.5 / math.sqrt(SIZE)
LOG2E = math.log2(math.e)
GELU_C = math.sqrt(2.0 / math.pi)
ABSENT = 8.0
ABSENT_ABOVE = 7.0
MASKED = -30000.0
GRAD_ROWS = 4096

bf16 = jnp.bfloat16
f32 = jnp.float32


def dot_nn(a, b):
    return lax.dot_general(a, b, (((1,), (0,)), ((), ())), preferred_element_type=f32)


def dot_nt(a, b):
    return lax.dot_general(a, b, (((1,), (1,)), ((), ())), preferred_element_type=f32)


def dot_tn(a, b):
    return lax.dot_general(a, b, (((0,), (0,)), ((), ())), preferred_element_type=f32)


def pick_kernel(asked_ref, cells_ref, out_ref, sem):
    def body(slot, carry):
        pltpu.make_async_copy(
            cells_ref.at[jnp.maximum(asked_ref[slot], 0)], out_ref.at[slot], sem
        ).start()
        return carry

    lax.fori_loop(0, out_ref.shape[0], body, 0)
    pltpu.make_async_copy(out_ref, out_ref, sem).wait()


def add_terms(asked_ref, back_ref, acc_ref):
    def body(slot, carry):
        asked = asked_ref[slot]

        @pl.when(asked >= 0)
        def _():
            acc_ref[asked] += back_ref[slot, : acc_ref.shape[1]].astype(f32)

        return carry

    lax.fori_loop(0, back_ref.shape[0], body, 0)


def sum_kernel(asked_ref, zero_ref, one_ref, zero_acc, one_acc):
    for ref, acc in ((zero_ref, zero_acc), (one_ref, one_acc)):
        acc[...] = jnp.zeros(acc.shape, f32)
        add_terms(asked_ref, ref, acc)


def last_kernel(asked_ref, zero_ref, one_ref, back_ref, out_ref, acc_ref):
    acc_ref[...] = jnp.zeros_like(acc_ref)
    add_terms(asked_ref, back_ref, acc_ref)
    zero, one, two = zero_ref[...], one_ref[...], acc_ref[...]
    out_ref[:, :, 0:128] = zero[:, :BLK].astype(bf16)
    out_ref[:, :, 128:256] = jnp.concatenate([zero[:, BLK:], one[:, :32]], axis=1).astype(bf16)
    out_ref[:, :, 256:384] = jnp.concatenate([one[:, 32:], two], axis=1).astype(bf16)


def mean_e(x):
    return jnp.sum(x, axis=-1, keepdims=True) * (1.0 / E)


def head_blocks(full):
    return jnp.concatenate(
        [full[SIZE * h : SIZE * (h + 1), 128 * h : 128 * (h + 1)] for h in range(H)]
        + [jnp.zeros((W - E, 128), f32)],
        axis=0,
    )


def spread_columns(tall, last):
    row = lax.broadcasted_iota(jnp.int32, tall.shape, 0)
    parts = []
    for h in range(H):
        inside = (row >= SIZE * h) & (row < SIZE * (h + 1))
        part = jnp.where(inside, tall, 0.0)
        if last:
            part = jnp.where(row == E, 1.0, part)
        parts.append(part)
    return jnp.concatenate(parts, axis=1).astype(bf16)


def spread_rows(wide):
    lane = lax.broadcasted_iota(jnp.int32, wide.shape, 1)
    parts = []
    for h in range(H):
        inside = (lane >= SIZE * h) & (lane < SIZE * (h + 1))
        parts.append(jnp.where(inside, wide, 0.0))
    return jnp.concatenate(parts, axis=0).astype(bf16)


def layer_norm(x, lane_in):
    centred = jnp.where(lane_in, x - mean_e(x), 0.0)
    scale = lax.rsqrt(mean_e(centred * centred) + 1e-05)
    return centred * scale, scale


def layer_norm_back(hat, scale, gain, dy):
    u = dy * gain
    return scale * (u - mean_e(u) - hat * mean_e(u * hat))


def rms_back(pre, scale, gain, dy):
    u = dy * gain
    return scale * (u - pre * (scale * scale) * mean_e(pre * u))


def feature_lanes(f):
    return slice(128 * f, 128 * f + W)


def side_by_side(first, second):
    return jnp.concatenate(
        [first[:, :128], first[:, 128:] + second[:, :128], second[:, 128:]], axis=1
    )


def widen(x, cols):
    return jnp.concatenate([x, jnp.zeros((x.shape[0], cols - x.shape[1]), x.dtype)], axis=1)


def heighten(x, rows):
    return jnp.concatenate([x, jnp.zeros((rows - x.shape[0], x.shape[1]), x.dtype)], axis=0)


def prepare_kernel(
    test_ref,
    cot_ref,
    w_query_ref,
    w_key_ref,
    w_value_ref,
    w_out_ref,
    w_up_ref,
    w_down_t_ref,
    q_gain_ref,
    k_gain_ref,
    gain_one_ref,
    gain_two_ref,
    projections_ref,
    ffn_ref,
    gains_ref,
    cells_ref,
    q_tall_ref,
):
    rows = test_ref.shape[0]
    row = lax.broadcasted_iota(jnp.int32, (E, W), 0)
    lane = lax.broadcasted_iota(jnp.int32, (E, W), 1)
    place = jnp.where(row == lane, 1.0, 0.0).astype(bf16)
    first = jnp.where((row == 0) & (lane == E), 1.0, 0.0).astype(bf16)
    nothing = jnp.zeros((W - E, W), bf16)
    weights = (
        widen(w_query_ref[...], W),
        widen(w_key_ref[...], W) + first,
        widen(w_value_ref[...], W),
        place,
    )
    for i, weight in enumerate(weights):
        for f in range(2):
            skip = f * (W - E)
            projections_ref[i, f, skip : skip + E, :] = weight
            projections_ref[i, f, (1 - f) * E : (1 - f) * E + W - E, :] = nothing
    ffn_ref[:, :FFH] = heighten(w_up_ref[...], W)
    ffn_ref[:, FFH : 2 * FFH] = heighten(w_down_t_ref[...], W)
    ffn_ref[:, 2 * FFH :] = heighten(widen(w_out_ref[...], W), W)
    for i, ref in enumerate((q_gain_ref, k_gain_ref, gain_one_ref, gain_two_ref)):
        gains_ref[i : i + 1, :] = widen(ref[...], W)
    test = test_ref[...]
    cot = cot_ref[...]
    q_gain = gains_ref[0:1, :]
    for f in range(2):
        here = slice(f * rows, (f + 1) * rows)
        lanes = feature_lanes(f)
        cells_ref[0, here, :] = dot_nn(test[:, lanes], projections_ref[3, f])
        cells_ref[1, here, :] = dot_nn(cot[:, lanes], projections_ref[3, f])
        pre = dot_nn(test[:, lanes], projections_ref[0, f])
        norm = pre * lax.rsqrt(mean_e(pre * pre) + 1e-06) * q_gain
        norm = norm.astype(bf16).astype(f32)
        q_tall_ref[f] = spread_columns(norm.T, True)


def main_kernel(
    tile,
    owner_ref,
    core_ref,
    rec_hbm,
    projections_hbm,
    ffn_hbm,
    gains_hbm,
    cells_hbm,
    q_tall_hbm,
    out_ref,
    grad_test_ref,
    zero_hbm,
    one_hbm,
    two_hbm,
    keep_hbm,
    give_hbm,
    projections_ref,
    ffn_ref,
    gains_ref,
    cells_ref,
    q_tall_ref,
    cells_s,
    kp_s,
    k_s,
    v_s,
    e_s,
    p_s,
    ds_s,
    d_s,
    grads_ref,
    zero_ref,
    one_ref,
    two_ref,
    rec_sem,
    sems,
):
    count = owner_ref.shape[0]
    feats = 2
    rows = out_ref.shape[0]
    keys = count * BLK

    def gather(j, carry):
        pltpu.make_async_copy(
            rec_hbm.at[owner_ref[j]],
            cells_s.at[pl.ds(pl.multiple_of(j * BLK, BLK), BLK), :],
            rec_sem,
        ).start()
        return carry

    lax.fori_loop(0, count, gather, 0)
    copies = [
        pltpu.make_async_copy(source, target, sems.at[i])
        for i, (source, target) in enumerate(
            (
                (projections_hbm, projections_ref),
                (gains_hbm, gains_ref),
                (q_tall_hbm, q_tall_ref),
                (cells_hbm, cells_ref),
                (ffn_hbm, ffn_ref),
            )
        )
    ]
    for copy in copies:
        copy.start()
    zero_ref[...] = jnp.zeros_like(zero_ref)
    one_ref[...] = jnp.zeros_like(one_ref)
    two_ref[...] = jnp.zeros_like(two_ref)
    pltpu.make_async_copy(cells_s, cells_s, rec_sem).wait()
    for copy in copies[:3]:
        copy.wait()

    q_gain = gains_ref[0:1, :]
    k_gain = gains_ref[1:2, :]
    gain_one = gains_ref[2:3, :]
    gain_two = gains_ref[3:4, :]

    tiles = [slice(t * tile, (t + 1) * tile) for t in range(keys // tile)]
    totals = []
    for f in range(feats):
        total = jnp.zeros((8, H * rows), f32)
        for here in tiles:
            cells = cells_s[here, feature_lanes(f)]
            pre = dot_nn(cells, projections_ref[1, f])
            lane = lax.broadcasted_iota(jnp.int32, pre.shape, 1)
            body = jnp.where(lane < E, pre, 0.0)
            scale = lax.rsqrt(mean_e(body * body) + 1e-06)
            bias = jnp.where((lane == E) & (pre > ABSENT_ABOVE), MASKED, 0.0)
            norm = (body * scale * k_gain + bias).astype(bf16)
            kp_s[f, here, :] = body
            k_s[f, here, :] = norm
            v_s[f, here, :] = dot_nn(cells, projections_ref[2, f]).astype(bf16)
            e = jnp.exp2(dot_nn(norm, q_tall_ref[f]) * (TEMPER * LOG2E))
            e_s[f, here, :] = e
            total = total + jnp.sum(e.reshape(tile // 8, 8, H * rows), axis=0)
        totals.append(jnp.sum(total, axis=0, keepdims=True))
    inverse = [1.0 / total for total in totals]
    inverse_tempered = [TEMPER / total for total in totals]
    mixed = []
    for f in range(feats):
        for here in tiles:
            p_s[f, here, :] = (e_s[f, here, :] * inverse[f]).astype(bf16)
        mixed.append(dot_tn(v_s[f, :, :E], p_s[f]))
    attended_t = [head_blocks(m) for m in mixed]

    for copy in copies[3:]:
        copy.wait()
    attended = jnp.concatenate([a.T for a in attended_t], axis=0).astype(bf16)
    lane_in = lax.broadcasted_iota(jnp.int32, (feats * rows, W), 1) < E
    w_up = ffn_ref[:, :FFH]
    w_down_t = ffn_ref[:, FFH : 2 * FFH]
    w_out = ffn_ref[:, 2 * FFH :]
    inner_one = cells_ref[0] + dot_nn(attended, w_out)
    hat_one, scale_one = layer_norm(inner_one, lane_in)
    normed_one = (hat_one * gain_one).astype(bf16)
    pre = dot_nn(normed_one, w_up)
    tanh = jnp.tanh(GELU_C * (pre + 0.044715 * (pre * pre * pre)))
    hidden = (0.5 * pre * (1.0 + tanh)).astype(bf16)
    slope = 0.5 * (1.0 + tanh) + (0.5 * GELU_C) * pre * (1.0 - tanh * tanh) * (
        1.0 + (3 * 0.044715) * (pre * pre)
    )
    inner_two = normed_one.astype(f32) + dot_nt(hidden, w_down_t)
    hat_two, scale_two = layer_norm(inner_two, lane_in)
    out = (hat_two * gain_two).astype(bf16)
    out_ref[...] = side_by_side(
        dot_nt(out[:rows], projections_ref[3, 0]), dot_nt(out[rows:], projections_ref[3, 1])
    ).astype(bf16)
    d_two = layer_norm_back(hat_two, scale_two, gain_two, cells_ref[1])
    d_two = jnp.where(lane_in, d_two, 0.0)
    d_two_b = d_two.astype(bf16)
    d_pre_b = (dot_nn(d_two_b, w_down_t) * slope).astype(bf16)
    d_normed = d_two + dot_nt(d_pre_b, w_up)
    d_one = layer_norm_back(hat_one, scale_one, gain_one, d_normed)
    d_one = jnp.where(lane_in, d_one, 0.0)
    d_one_b = d_one.astype(bf16)
    d_att = dot_nt(d_one_b, w_out).astype(bf16).astype(f32)
    put_grads(grads_ref, 6, dot_tn(attended, d_one_b)[:E])
    put_grads(grads_ref, 8, dot_tn(normed_one, d_pre_b)[:E])
    put_grads(grads_ref, 14, dot_tn(d_two_b, hidden)[:E])

    da_t, da_rows, dots = [], [], []
    q_cells, q_pre, q_scale, q_rows = [], [], [], []
    for f in range(feats):
        cells = cells_ref[0, f * rows : (f + 1) * rows, :].astype(bf16)
        pre = dot_nn(cells, projections_ref[0, 0])
        scale = lax.rsqrt(mean_e(pre * pre) + 1e-06)
        q_cells.append(cells)
        q_pre.append(pre)
        q_scale.append(scale)
        q_rows.append(spread_rows((pre * scale * q_gain).astype(bf16).astype(f32)))
        mine = d_att[f * rows : (f + 1) * rows]
        mine_t = mine.T
        da_t.append(spread_columns(mine_t, False))
        da_rows.append(spread_rows(mine))
        product = mine_t * attended_t[f]
        dots.append(
            jnp.concatenate(
                [
                    jnp.sum(product[SIZE * h : SIZE * (h + 1)], axis=0, keepdims=True)
                    for h in range(H)
                ],
                axis=1,
            )
        )

    d_queries = []
    for f in range(feats):
        for here in tiles:
            grad_w = dot_nn(v_s[f, here, :], da_t[f])
            probs = e_s[f, here, :] * inverse_tempered[f]
            ds_s[f, here, :] = (probs * (grad_w - dots[f])).astype(bf16)
        d_queries.append(dot_tn(k_s[f, :, :E], ds_s[f]))
    for t, here in enumerate(tiles):
        d_cells = []
        for f in range(feats):
            d_key = dot_nn(ds_s[f, here, :], q_rows[f])
            d_value = dot_nn(p_s[f, here, :], da_rows[f]).astype(bf16)
            body = kp_s[f, here, :]
            scale = lax.rsqrt(mean_e(body * body) + 1e-06)
            d_kpre = rms_back(body, scale, k_gain, d_key).astype(bf16)
            d_s[here, 2 * f * W : (2 * f + 1) * W] = d_kpre
            d_s[here, (2 * f + 1) * W : (2 * f + 2) * W] = d_value
            d_cells.append(
                dot_nt(d_kpre, projections_ref[1, f]) + dot_nt(d_value, projections_ref[2, f])
            )
        d_cells = side_by_side(*d_cells).astype(bf16)
        for b in range(tile // BLK):
            owner = owner_ref[t * (tile // BLK) + b]
            block = d_cells[b * BLK : (b + 1) * BLK]
            zero_ref[owner, :BLK] = block[:, :128]
            zero_ref[owner, BLK:] = block[:32, 128:256]
            one_ref[owner, :32] = block[32:, 128:256]
            one_ref[owner, 32:] = block[:16, 256:]
            two_ref[owner] = block[16:, 256:]

    sends = [
        pltpu.make_async_copy(source, target, sems.at[i])
        for i, (source, target) in enumerate(
            ((zero_ref, zero_hbm), (one_ref, one_hbm), (two_ref, two_hbm))
        )
    ]
    for copy in sends:
        copy.start()

    d_test = []
    g_query = jnp.zeros((W, W), f32)
    placed = []
    for f in range(feats):
        here = slice(f * rows, (f + 1) * rows)
        d_query = head_blocks(d_queries[f]).T
        d_qpre = rms_back(q_pre[f], q_scale[f], q_gain, d_query).astype(bf16)
        g_query = g_query + dot_tn(q_cells[f], d_qpre)
        d_test.append(dot_nt(d_qpre, projections_ref[0, f]))
        placed.append(d_one[here, :E])
    grad_test_ref[...] = (side_by_side(*d_test) + jnp.concatenate(placed, axis=1)).astype(bf16)
    put_grads(grads_ref, 0, g_query[:E])
    kv = jnp.zeros((E, 2 * W), f32)
    for f in range(feats):
        both = dot_tn(cells_s[:, feature_lanes(f)], d_s[:, 2 * f * W : 2 * (f + 1) * W])
        kv = kv + both[f * (W - E) : f * (W - E) + E]
    put_grads(grads_ref, 2, kv)
    grads_ref[20 * E :, :] = jnp.zeros((GRAD_ROWS - 20 * E, 128), bf16)
    core = core_ref[0]
    for i, (half, target) in enumerate(((core, keep_hbm), (1 - core, give_hbm))):
        start = pl.multiple_of(half * (GRAD_ROWS // 2), 128)
        copy = pltpu.make_async_copy(
            grads_ref.at[pl.ds(start, GRAD_ROWS // 2), :], target, sems.at[len(sends)]
        )
        copy.start()
        sends.append(copy)
    for copy in sends:
        copy.wait()


def put_grads(grads_ref, first, value):
    for i in range(value.shape[1] // 128):
        rows = slice((first + i) * E, (first + i + 1) * E)
        grads_ref[rows, :] = value[:, 128 * i : 128 * (i + 1)].astype(bf16)


def take_grads(ref, first, pieces):
    return jnp.concatenate(
        [ref[(first + i) * E : (first + i + 1) * E, :].astype(f32) for i in range(pieces)], axis=1
    )


def halve_kernel(bit_ref, keep_ref, got_ref, next_keep_ref, next_give_ref):
    half = next_keep_ref.shape[0]
    bit = bit_ref[0]
    for part, ref in ((bit, next_keep_ref), (1 - bit, next_give_ref)):
        rows = pl.ds(pl.multiple_of(part * half, 128), half)
        ref[...] = (keep_ref[rows, :].astype(f32) + got_ref[rows, :].astype(f32)).astype(bf16)


def ride_kernel(keep_ref, got_ref, one_ref, earlier_ref, out_ref):
    cut = one_ref.shape[1]
    total = (keep_ref[...].astype(f32) + got_ref[...].astype(f32)).astype(bf16)
    out_ref[:, :cut, :] = one_ref[...]
    out_ref[:, cut:, :] = total.reshape(out_ref.shape[0], out_ref.shape[1] - cut, 128)


def ride_back_kernel(back_ref, two_ref, out_ref):
    cut = two_ref.shape[1]
    total = jnp.sum(back_ref[:, cut:, :].astype(f32), axis=0).astype(bf16)
    out_ref[:, :cut, :] = two_ref[...]
    out_ref[:, cut:, :] = jnp.broadcast_to(total[None], out_ref[:, cut:, :].shape)


def share_kernel(back_ref, zero_ref, one_ref, out_ref):
    pieces = out_ref.shape[1] // back_ref.shape[0]
    share = back_ref[:, back_ref.shape[1] - pieces :, :].reshape(out_ref.shape[1], 128)
    out_ref[...] = jnp.broadcast_to(share[None], out_ref.shape)


def unpack_kernel(
    core_ref, mine_ref, got_ref, query_ref, key_ref, value_ref, w_out_ref, up_ref, down_t_ref, all_ref
):
    chips, share, _ = mine_ref.shape
    core = core_ref[0]
    for half, ref in ((core, mine_ref), (1 - core, got_ref)):
        for chip in range(chips):
            place = (chip % 2) * 2 + chip // 2
            start = pl.multiple_of(half * (chips * share) + place * share, 128)
            all_ref[pl.ds(start, share), :] = ref[chip]
    for i, ref in enumerate((query_ref, key_ref, value_ref, w_out_ref)):
        ref[...] = take_grads(all_ref, 2 * i, 2)[:, :E]
    up_ref[...] = take_grads(all_ref, 8, 6)
    down_t_ref[...] = take_grads(all_ref, 14, 6)


def vmem_specs(n):
    return [pl.BlockSpec(memory_space=pltpu.VMEM)] * n


SMEM_SPEC = pl.BlockSpec(memory_space=pltpu.SMEM)
MIB = 1024 * 1024


BUSY = pl.CostEstimate(flops=10**9, bytes_accessed=4 * MIB, transcendentals=0)
ANY_SPEC = pl.BlockSpec(memory_space=pl.ANY)
HBM_SPEC = pl.BlockSpec(memory_space=pltpu.HBM)
PARAMS = pltpu.CompilerParams(vmem_limit_bytes=12 * MIB)
MAIN_PARAMS = pltpu.CompilerParams(vmem_limit_bytes=62 * MIB)


def shape(dims, dtype=bf16):
    return jax.ShapeDtypeStruct(dims, dtype)


def small_call(kernel, out_shape, *args, scalars=(), scratch=(), cost=None):
    return pl.pallas_call(
        kernel,
        out_shape=out_shape,
        in_specs=[SMEM_SPEC] * len(scalars) + vmem_specs(len(args)),
        out_specs=jax.tree.map(lambda _: vmem_specs(1)[0], out_shape),
        scratch_shapes=scratch,
        compiler_params=PARAMS,
        cost_estimate=cost,
    )(*scalars, *args)


def prepare(test_cells, cotangent, weights):
    w_query, q_gain, w_key, k_gain, w_value, w_out, gain_one, w_up, w_down, gain_two = weights
    rows, wide = test_cells.shape
    ht = H * rows
    shapes = (
        shape((4, 2, W, W)),
        shape((W, 2 * FFH + W)),
        shape((4, W), f32),
        shape((2, 2 * rows, W), f32),
        shape((2, W, ht)),
    )
    args = (test_cells, cotangent, w_query, w_key, w_value, w_out, w_up, w_down.T) + tuple(
        gain.reshape(1, E) for gain in (q_gain, k_gain, gain_one, gain_two)
    )
    return small_call(prepare_kernel, shapes, *args)


def main_call(owner_of, core, rec, prepared, rows, tile):
    count = owner_of.shape[0]
    keys = count * BLK
    owners, _, wide = rec.shape
    ht = H * rows
    return pl.pallas_call(
        functools.partial(main_kernel, tile),
        out_shape=(
            shape((rows, wide)),
            shape((rows, wide)),
            pltpu.HBM((owners, 96, 128), bf16),
            pltpu.HBM((owners, 48, 128), bf16),
            pltpu.HBM((owners, 48, 128), bf16),
            pltpu.HBM((GRAD_ROWS // 2, 128), bf16),
            pltpu.HBM((GRAD_ROWS // 2, 128), bf16),
        ),
        in_specs=[SMEM_SPEC] * 2 + [HBM_SPEC] * (1 + len(prepared)),
        out_specs=tuple(vmem_specs(2)) + (HBM_SPEC,) * 5,
        scratch_shapes=[pltpu.VMEM(x.shape, x.dtype) for x in prepared]
        + [
            pltpu.VMEM((keys, wide), bf16),
            pltpu.VMEM((2, keys, W), f32),
            pltpu.VMEM((2, keys, W), bf16),
            pltpu.VMEM((2, keys, W), bf16),
            pltpu.VMEM((2, keys, ht), f32),
            pltpu.VMEM((2, keys, ht), bf16),
            pltpu.VMEM((2, keys, ht), bf16),
            pltpu.VMEM((keys, 4 * W), bf16),
            pltpu.VMEM((GRAD_ROWS, 128), bf16),
            pltpu.VMEM((owners, 96, 128), bf16),
            pltpu.VMEM((owners, 48, 128), bf16),
            pltpu.VMEM((owners, 48, 128), bf16),
            pltpu.SemaphoreType.DMA,
            pltpu.SemaphoreType.DMA((len(prepared),)),
        ],
        compiler_params=MAIN_PARAMS,
    )(owner_of, core, rec, *prepared)


def swap(x, axis):
    return lax.all_to_all(x, axis, split_axis=0, concat_axis=0, tiled=True)


def on_device(
    test_cells,
    train_cells,
    train_present,
    retrieved,
    w_query,
    q_gain,
    w_key,
    k_gain,
    w_value,
    w_out,
    gain_one,
    w_up,
    w_down,
    gain_two,
    cotangent,
):
    owners, groups = lax.axis_size("rows"), lax.axis_size("feat")
    blocks_own = train_cells.shape[0] // BLK
    rows, wide = test_cells.shape
    count = retrieved.shape[1]
    owner_of = retrieved[0] // blocks_own
    table = swap(jnp.broadcast_to(retrieved[None], (owners, 1, count)), "rows")
    table = table.reshape(owners, count)
    mine = table // blocks_own == lax.axis_index("rows")
    asked = jnp.sum(jnp.where(mine, table % blocks_own + 1, 0), axis=1) - 1
    mask = jnp.repeat(train_present.T != 0, E, axis=1)
    marked = jnp.where(mask, train_cells, jnp.asarray(ABSENT, bf16)).reshape(blocks_own, BLK, wide)
    to_send = pl.pallas_call(
        pick_kernel,
        out_shape=shape((owners, BLK, wide)),
        in_specs=[SMEM_SPEC] + vmem_specs(1),
        out_specs=ANY_SPEC,
        scratch_shapes=[pltpu.SemaphoreType.DMA],
        compiler_params=PARAMS,
    )(asked, marked)
    rec = swap(to_send, "rows")
    prepared = prepare(
        test_cells,
        cotangent,
        (w_query, q_gain, w_key, k_gain, w_value, w_out, gain_one, w_up, w_down, gain_two),
    )
    feat = lax.axis_index("feat")
    core, low, high = ((feat // bit % 2).reshape(1) for bit in (1, 2, 4))
    out_cells, grad_test, zero, one, two, keep, give = main_call(
        owner_of, core, rec, prepared, rows, 1024
    )

    back_zero = swap(zero, "rows")
    got = flip(give, 1)
    half = keep.shape[0] // 2
    keep, give = small_call(halve_kernel, (shape((half, 128)),) * 2, keep, got, scalars=(low,))
    got = flip(give, 2)
    half = half // 2
    keep, give = small_call(halve_kernel, (shape((half, 128)),) * 2, keep, got, scalars=(high,))
    got = flip(give, 4)
    piece = half // owners
    riding = shape((owners, one.shape[1] + piece, 128))
    ride = pl.pallas_call(
        ride_kernel,
        out_shape=riding,
        in_specs=vmem_specs(3) + [ANY_SPEC],
        out_specs=vmem_specs(1)[0],
        compiler_params=PARAMS,
    )(keep, got, one, back_zero)
    back_one = swap(ride, "rows")
    back_two = swap(small_call(ride_back_kernel, riding, back_one, two), "rows")
    chips = groups // 2
    sums = small_call(
        sum_kernel,
        tuple(shape((blocks_own, x.shape[1], 128), f32) for x in (zero, one)),
        back_zero,
        back_one,
        scalars=(asked,),
        cost=BUSY,
    )
    copies = pl.pallas_call(
        share_kernel,
        out_shape=shape((chips, half, 128)),
        in_specs=vmem_specs(1) + [ANY_SPEC] * 2,
        out_specs=vmem_specs(1)[0],
        compiler_params=PARAMS,
    )(back_two, *sums)
    mine = lax.all_to_all(
        copies,
        "feat",
        split_axis=0,
        concat_axis=0,
        tiled=True,
        axis_index_groups=[[2 * chip + c for chip in range(chips)] for c in range(2)],
    )
    others = flip(mine, 1)
    grad_train = small_call(
        last_kernel,
        shape((blocks_own, BLK, wide)),
        *sums,
        back_two,
        scalars=(asked,),
        scratch=[pltpu.VMEM((blocks_own, two.shape[1], 128), f32)],
        cost=BUSY,
    ).reshape(blocks_own * BLK, wide)
    *weights, g_down_t = unpack(core, mine, others)
    return (out_cells, grad_test, grad_train, *weights, g_down_t.T)


def flip(x, bit):
    count = lax.axis_size("feat")
    return lax.ppermute(x, "feat", [(i, i ^ bit) for i in range(count)])


def unpack(core, mine, others):
    return small_call(
        unpack_kernel,
        (shape((E, E), f32),) * 4 + (shape((E, FFH), f32),) * 2,
        mine,
        others,
        scalars=(core,),
        scratch=[pltpu.VMEM((GRAD_ROWS, 128), bf16)],
    )


def solution(mesh):
    in_specs = (
        P("rows", "feat"),
        P("rows", "feat"),
        P("feat", "rows"),
        P("rows", None),
        P(),
        P(),
        P(),
        P(),
        P(),
        P(),
        P(),
        P(),
        P(),
        P(),
        P("rows", "feat"),
    )
    out_specs = (
        P("rows", "feat"),
        P("rows", "feat"),
        P("rows", "feat"),
        P(),
        P(),
        P(),
        P(),
        P(),
        P(),
    )
    return jax.shard_map(
        on_device, mesh=mesh, in_specs=in_specs, out_specs=out_specs, check_vma=False
    )
```

```python
import functools
import math

import jax
import jax.numpy as jnp
from jax import lax
from jax.experimental import pallas as pl
from jax.experimental.pallas import tpu as pltpu
from jax.sharding import PartitionSpec as P

H = 6
BLK = 64
E = 192
W = 256
FFH = 768
SIZE = E // H
TEMPER = 1.5 / math.sqrt(SIZE)
LOG2E = math.log2(math.e)
GELU_C = math.sqrt(2.0 / math.pi)
ABSENT = 8.0
ABSENT_ABOVE = 7.0
MASKED = -30000.0
GRAD_ROWS = 4096
Z = 8

bf16 = jnp.bfloat16
f32 = jnp.float32


def dot_nn(a, b):
    return lax.dot_general(a, b, (((1,), (0,)), ((), ())), preferred_element_type=f32)


def dot_nt(a, b):
    return lax.dot_general(a, b, (((1,), (1,)), ((), ())), preferred_element_type=f32)


def dot_tn(a, b):
    return lax.dot_general(a, b, (((0,), (0,)), ((), ())), preferred_element_type=f32)


def mark_kernel(
    train_hbm,
    present_hbm,
    retrieved_hbm,
    marked_ref,
    requests_ref,
    train_ref,
    present_ref,
    retrieved_ref,
    sems,
):
    copies = [
        pltpu.make_async_copy(source, target, sems.at[i])
        for i, (source, target) in enumerate(
            ((train_hbm, train_ref), (present_hbm, present_ref), (retrieved_hbm, retrieved_ref))
        )
    ]
    for copy in copies:
        copy.start()
    for copy in copies:
        copy.wait()
    wide = train_ref.shape[1]
    feats, rows = present_ref.shape
    present = jnp.concatenate(
        [present_ref[...].astype(f32), jnp.zeros((16 - feats, rows), f32)], axis=0
    ).astype(bf16)
    feature = lax.broadcasted_iota(jnp.int32, (16, wide), 0)
    lane = lax.broadcasted_iota(jnp.int32, (16, wide), 1)
    mine = (lane >= feature * E) & (lane < (feature + 1) * E)
    mask = dot_tn(present, jnp.where(mine, 1.0, 0.0).astype(bf16))
    marked = jnp.where(mask > 0.5, train_ref[...].astype(f32), ABSENT).astype(bf16)
    marked_ref[...] = marked.reshape(marked_ref.shape)
    requests_ref[...] = jnp.broadcast_to(retrieved_ref[...][None], requests_ref.shape)


def arrived_kernel(in_ref, out_ref):
    pass


def asked_kernel(blocks, served_ref, table_ref, mirrored_ref, out_ref):
    table = table_ref[:, 0, :]
    owner = lax.div(table, blocks)
    wanted = lax.rem(table, blocks) + 1
    part = lax.broadcasted_iota(jnp.int32, out_ref.shape, 1)
    own, mirrored = (
        jnp.sum(jnp.where(owner == served_ref[i], wanted, 0), axis=1, keepdims=True) - 1
        for i in range(2)
    )
    out_ref[...] = jnp.where(part == 0, own, mirrored)


def pick_kernel(asked_ref, base_ref, own_ref, mirrored_ref, out_ref, sem):
    def body(k, carry):
        row = (k // 4) * Z + lax.rem(base_ref[0] + lax.rem(k, 4), Z)
        for part, ref in enumerate((own_ref, mirrored_ref)):
            pltpu.make_async_copy(
                ref.at[jnp.maximum(asked_ref[row, part], 0)], out_ref.at[k, part], sem
            ).start()
        return carry

    lax.fori_loop(0, out_ref.shape[0], body, 0)
    pltpu.make_async_copy(out_ref, out_ref, sem).wait()


def add_terms(asked_ref, back_ref, acc_ref):
    def body(slot, carry):
        asked = asked_ref[slot]

        @pl.when(asked >= 0)
        def _():
            acc_ref[asked] += back_ref[slot, : acc_ref.shape[1]].astype(f32)

        return carry

    lax.fori_loop(0, back_ref.shape[0], body, 0)


def sum_kernel(asked_ref, zero_ref, one_ref, zero_acc, one_acc):
    for ref, acc in ((zero_ref, zero_acc), (one_ref, one_acc)):
        acc[...] = jnp.zeros(acc.shape, f32)
        add_terms(asked_ref, ref, acc)


def last_kernel(asked_ref, zero_ref, one_ref, back_ref, out_ref, acc_ref):
    acc_ref[...] = jnp.zeros_like(acc_ref)
    add_terms(asked_ref, back_ref, acc_ref)
    zero, one, two = zero_ref[...], one_ref[...], acc_ref[...]
    out_ref[:, :, 0:128] = zero[:, :BLK].astype(bf16)
    out_ref[:, :, 128:256] = jnp.concatenate([zero[:, BLK:], one[:, :32]], axis=1).astype(bf16)
    out_ref[:, :, 256:384] = jnp.concatenate([one[:, 32:], two], axis=1).astype(bf16)


def mean_e(x):
    return jnp.sum(x, axis=-1, keepdims=True) * (1.0 / E)


def head_blocks(full):
    return jnp.concatenate(
        [full[SIZE * h : SIZE * (h + 1), 128 * h : 128 * (h + 1)] for h in range(H)]
        + [jnp.zeros((W - E, 128), f32)],
        axis=0,
    )


def spread_columns(tall, last):
    row = lax.broadcasted_iota(jnp.int32, tall.shape, 0)
    parts = []
    for h in range(H):
        inside = (row >= SIZE * h) & (row < SIZE * (h + 1))
        part = jnp.where(inside, tall, 0.0)
        if last:
            part = jnp.where(row == E, 1.0, part)
        parts.append(part)
    return jnp.concatenate(parts, axis=1).astype(bf16)


def spread_rows(wide):
    lane = lax.broadcasted_iota(jnp.int32, wide.shape, 1)
    parts = []
    for h in range(H):
        inside = (lane >= SIZE * h) & (lane < SIZE * (h + 1))
        parts.append(jnp.where(inside, wide, 0.0))
    return jnp.concatenate(parts, axis=0).astype(bf16)


def layer_norm(x, lane_in):
    centred = jnp.where(lane_in, x - mean_e(x), 0.0)
    scale = lax.rsqrt(mean_e(centred * centred) + 1e-05)
    return centred * scale, scale


def layer_norm_back(hat, scale, gain, dy):
    u = dy * gain
    return scale * (u - mean_e(u) - hat * mean_e(u * hat))


def rms_back(pre, scale, gain, dy):
    u = dy * gain
    return scale * (u - pre * (scale * scale) * mean_e(pre * u))


def feature_lanes(f):
    return slice(128 * f, 128 * f + W)


def side_by_side(first, second):
    return jnp.concatenate(
        [first[:, :128], first[:, 128:] + second[:, :128], second[:, 128:]], axis=1
    )


def widen(x, cols):
    return jnp.concatenate([x, jnp.zeros((x.shape[0], cols - x.shape[1]), x.dtype)], axis=1)


def heighten(x, rows):
    return jnp.concatenate([x, jnp.zeros((rows - x.shape[0], x.shape[1]), x.dtype)], axis=0)


def prepare_kernel(
    asked_ref,
    test_ref,
    cot_ref,
    w_query_ref,
    w_key_ref,
    w_value_ref,
    w_out_ref,
    w_up_ref,
    w_down_t_ref,
    q_gain_ref,
    k_gain_ref,
    gain_one_ref,
    gain_two_ref,
    projections_ref,
    ffn_ref,
    gains_ref,
    cells_ref,
    q_tall_ref,
):
    rows = test_ref.shape[0]
    row = lax.broadcasted_iota(jnp.int32, (E, W), 0)
    lane = lax.broadcasted_iota(jnp.int32, (E, W), 1)
    place = jnp.where(row == lane, 1.0, 0.0).astype(bf16)
    first = jnp.where((row == 0) & (lane == E), 1.0, 0.0).astype(bf16)
    nothing = jnp.zeros((W - E, W), bf16)
    weights = (
        widen(w_query_ref[...], W),
        widen(w_key_ref[...], W) + first,
        widen(w_value_ref[...], W),
        place,
    )
    for i, weight in enumerate(weights):
        for f in range(2):
            skip = f * (W - E)
            projections_ref[i, f, skip : skip + E, :] = weight
            projections_ref[i, f, (1 - f) * E : (1 - f) * E + W - E, :] = nothing
    ffn_ref[:, :FFH] = heighten(w_up_ref[...], W)
    ffn_ref[:, FFH : 2 * FFH] = heighten(w_down_t_ref[...], W)
    ffn_ref[:, 2 * FFH :] = heighten(widen(w_out_ref[...], W), W)
    for i, ref in enumerate((q_gain_ref, k_gain_ref, gain_one_ref, gain_two_ref)):
        gains_ref[i : i + 1, :] = widen(ref[...], W)
    test = test_ref[...]
    cot = cot_ref[...]
    q_gain = gains_ref[0:1, :]
    for f in range(2):
        here = slice(f * rows, (f + 1) * rows)
        lanes = feature_lanes(f)
        cells_ref[0, here, :] = dot_nn(test[:, lanes], projections_ref[3, f])
        cells_ref[1, here, :] = dot_nn(cot[:, lanes], projections_ref[3, f])
        pre = dot_nn(test[:, lanes], projections_ref[0, f])
        norm = pre * lax.rsqrt(mean_e(pre * pre) + 1e-06) * q_gain
        norm = norm.astype(bf16).astype(f32)
        q_tall_ref[f] = spread_columns(norm.T, True)


def main_kernel(
    tile,
    source_ref,
    owner_ref,
    core_ref,
    rec_hbm,
    projections_hbm,
    ffn_hbm,
    gains_hbm,
    cells_hbm,
    q_tall_hbm,
    out_ref,
    grad_test_ref,
    zero_hbm,
    one_hbm,
    two_hbm,
    keep_hbm,
    give_hbm,
    projections_ref,
    ffn_ref,
    gains_ref,
    cells_ref,
    q_tall_ref,
    cells_s,
    kp_s,
    k_s,
    v_s,
    e_s,
    p_s,
    ds_s,
    d_s,
    grads_ref,
    zero_ref,
    one_ref,
    two_ref,
    rec_sem,
    sems,
):
    count = owner_ref.shape[0]
    feats = 2
    rows = out_ref.shape[0]
    keys = count * BLK

    def gather(j, carry):
        pltpu.make_async_copy(
            rec_hbm.at[source_ref[j]],
            cells_s.at[pl.ds(pl.multiple_of(j * BLK, BLK), BLK), :],
            rec_sem,
        ).start()
        return carry

    lax.fori_loop(0, count, gather, 0)
    copies = [
        pltpu.make_async_copy(source, target, sems.at[i])
        for i, (source, target) in enumerate(
            (
                (projections_hbm, projections_ref),
                (gains_hbm, gains_ref),
                (q_tall_hbm, q_tall_ref),
                (cells_hbm, cells_ref),
                (ffn_hbm, ffn_ref),
            )
        )
    ]
    for copy in copies:
        copy.start()
    zero_ref[...] = jnp.zeros_like(zero_ref)
    one_ref[...] = jnp.zeros_like(one_ref)
    two_ref[...] = jnp.zeros_like(two_ref)
    pltpu.make_async_copy(cells_s, cells_s, rec_sem).wait()
    for copy in copies[:3]:
        copy.wait()

    q_gain = gains_ref[0:1, :]
    k_gain = gains_ref[1:2, :]
    gain_one = gains_ref[2:3, :]
    gain_two = gains_ref[3:4, :]

    tiles = [slice(t * tile, (t + 1) * tile) for t in range(keys // tile)]
    totals = []
    for f in range(feats):
        total = jnp.zeros((8, H * rows), f32)
        for here in tiles:
            cells = cells_s[here, feature_lanes(f)]
            pre = dot_nn(cells, projections_ref[1, f])
            lane = lax.broadcasted_iota(jnp.int32, pre.shape, 1)
            body = jnp.where(lane < E, pre, 0.0)
            scale = lax.rsqrt(mean_e(body * body) + 1e-06)
            bias = jnp.where((lane == E) & (pre > ABSENT_ABOVE), MASKED, 0.0)
            norm = (body * scale * k_gain + bias).astype(bf16)
            kp_s[f, here, :] = body
            k_s[f, here, :] = norm
            v_s[f, here, :] = dot_nn(cells, projections_ref[2, f]).astype(bf16)
            e = jnp.exp2(dot_nn(norm, q_tall_ref[f]) * (TEMPER * LOG2E))
            e_s[f, here, :] = e
            total = total + jnp.sum(e.reshape(tile // 8, 8, H * rows), axis=0)
        totals.append(jnp.sum(total, axis=0, keepdims=True))
    inverse = [1.0 / total for total in totals]
    inverse_tempered = [TEMPER / total for total in totals]
    mixed = []
    for f in range(feats):
        for here in tiles:
            p_s[f, here, :] = (e_s[f, here, :] * inverse[f]).astype(bf16)
        mixed.append(dot_tn(v_s[f, :, :E], p_s[f]))
    attended_t = [head_blocks(m) for m in mixed]

    for copy in copies[3:]:
        copy.wait()
    attended = jnp.concatenate([a.T for a in attended_t], axis=0).astype(bf16)
    lane_in = lax.broadcasted_iota(jnp.int32, (feats * rows, W), 1) < E
    w_up = ffn_ref[:, :FFH]
    w_down_t = ffn_ref[:, FFH : 2 * FFH]
    w_out = ffn_ref[:, 2 * FFH :]
    inner_one = cells_ref[0] + dot_nn(attended, w_out)
    hat_one, scale_one = layer_norm(inner_one, lane_in)
    normed_one = (hat_one * gain_one).astype(bf16)
    pre = dot_nn(normed_one, w_up)
    tanh = jnp.tanh(GELU_C * (pre + 0.044715 * (pre * pre * pre)))
    hidden = (0.5 * pre * (1.0 + tanh)).astype(bf16)
    slope = 0.5 * (1.0 + tanh) + (0.5 * GELU_C) * pre * (1.0 - tanh * tanh) * (
        1.0 + (3 * 0.044715) * (pre * pre)
    )
    inner_two = normed_one.astype(f32) + dot_nt(hidden, w_down_t)
    hat_two, scale_two = layer_norm(inner_two, lane_in)
    out = (hat_two * gain_two).astype(bf16)
    out_ref[...] = side_by_side(
        dot_nt(out[:rows], projections_ref[3, 0]), dot_nt(out[rows:], projections_ref[3, 1])
    ).astype(bf16)
    d_two = layer_norm_back(hat_two, scale_two, gain_two, cells_ref[1])
    d_two = jnp.where(lane_in, d_two, 0.0)
    d_two_b = d_two.astype(bf16)
    d_pre_b = (dot_nn(d_two_b, w_down_t) * slope).astype(bf16)
    d_normed = d_two + dot_nt(d_pre_b, w_up)
    d_one = layer_norm_back(hat_one, scale_one, gain_one, d_normed)
    d_one = jnp.where(lane_in, d_one, 0.0)
    d_one_b = d_one.astype(bf16)
    d_att = dot_nt(d_one_b, w_out).astype(bf16).astype(f32)
    put_grads(grads_ref, 6, dot_tn(attended, d_one_b)[:E])
    put_grads(grads_ref, 8, dot_tn(normed_one, d_pre_b)[:E])
    put_grads(grads_ref, 14, dot_tn(d_two_b, hidden)[:E])

    da_t, da_rows, dots = [], [], []
    q_cells, q_pre, q_scale, q_rows = [], [], [], []
    for f in range(feats):
        cells = cells_ref[0, f * rows : (f + 1) * rows, :].astype(bf16)
        pre = dot_nn(cells, projections_ref[0, 0])
        scale = lax.rsqrt(mean_e(pre * pre) + 1e-06)
        q_cells.append(cells)
        q_pre.append(pre)
        q_scale.append(scale)
        q_rows.append(spread_rows((pre * scale * q_gain).astype(bf16).astype(f32)))
        mine = d_att[f * rows : (f + 1) * rows]
        mine_t = mine.T
        da_t.append(spread_columns(mine_t, False))
        da_rows.append(spread_rows(mine))
        product = mine_t * attended_t[f]
        dots.append(
            jnp.concatenate(
                [
                    jnp.sum(product[SIZE * h : SIZE * (h + 1)], axis=0, keepdims=True)
                    for h in range(H)
                ],
                axis=1,
            )
        )

    d_queries = []
    for f in range(feats):
        for here in tiles:
            grad_w = dot_nn(v_s[f, here, :], da_t[f])
            probs = e_s[f, here, :] * inverse_tempered[f]
            ds_s[f, here, :] = (probs * (grad_w - dots[f])).astype(bf16)
        d_queries.append(dot_tn(k_s[f, :, :E], ds_s[f]))
    for t, here in enumerate(tiles):
        d_cells = []
        for f in range(feats):
            d_key = dot_nn(ds_s[f, here, :], q_rows[f])
            d_value = dot_nn(p_s[f, here, :], da_rows[f]).astype(bf16)
            body = kp_s[f, here, :]
            scale = lax.rsqrt(mean_e(body * body) + 1e-06)
            d_kpre = rms_back(body, scale, k_gain, d_key).astype(bf16)
            d_s[here, 2 * f * W : (2 * f + 1) * W] = d_kpre
            d_s[here, (2 * f + 1) * W : (2 * f + 2) * W] = d_value
            d_cells.append(
                dot_nt(d_kpre, projections_ref[1, f]) + dot_nt(d_value, projections_ref[2, f])
            )
        d_cells = side_by_side(*d_cells).astype(bf16)
        for b in range(tile // BLK):
            owner = owner_ref[t * (tile // BLK) + b]
            block = d_cells[b * BLK : (b + 1) * BLK]
            zero_ref[owner, :BLK] = block[:, :128]
            zero_ref[owner, BLK:] = block[:32, 128:256]
            one_ref[owner, :32] = block[32:, 128:256]
            one_ref[owner, 32:] = block[:16, 256:]
            two_ref[owner] = block[16:, 256:]

    sends = [
        pltpu.make_async_copy(source, target, sems.at[i])
        for i, (source, target) in enumerate(
            ((zero_ref, zero_hbm), (one_ref, one_hbm), (two_ref, two_hbm))
        )
    ]
    for copy in sends:
        copy.start()

    d_test = []
    g_query = jnp.zeros((W, W), f32)
    placed = []
    for f in range(feats):
        here = slice(f * rows, (f + 1) * rows)
        d_query = head_blocks(d_queries[f]).T
        d_qpre = rms_back(q_pre[f], q_scale[f], q_gain, d_query).astype(bf16)
        g_query = g_query + dot_tn(q_cells[f], d_qpre)
        d_test.append(dot_nt(d_qpre, projections_ref[0, f]))
        placed.append(d_one[here, :E])
    grad_test_ref[...] = (side_by_side(*d_test) + jnp.concatenate(placed, axis=1)).astype(bf16)
    put_grads(grads_ref, 0, g_query[:E])
    kv = jnp.zeros((E, 2 * W), f32)
    for f in range(feats):
        both = dot_tn(cells_s[:, feature_lanes(f)], d_s[:, 2 * f * W : 2 * (f + 1) * W])
        kv = kv + both[f * (W - E) : f * (W - E) + E]
    put_grads(grads_ref, 2, kv)
    grads_ref[20 * E :, :] = jnp.zeros((GRAD_ROWS - 20 * E, 128), bf16)
    core = core_ref[0]
    for i, (half, target) in enumerate(((core, keep_hbm), (1 - core, give_hbm))):
        start = pl.multiple_of(half * (GRAD_ROWS // 2), 128)
        copy = pltpu.make_async_copy(
            grads_ref.at[pl.ds(start, GRAD_ROWS // 2), :], target, sems.at[len(sends)]
        )
        copy.start()
        sends.append(copy)
    for copy in sends:
        copy.wait()


def put_grads(grads_ref, first, value):
    for i in range(value.shape[1] // 128):
        rows = slice((first + i) * E, (first + i + 1) * E)
        grads_ref[rows, :] = value[:, 128 * i : 128 * (i + 1)].astype(bf16)


def take_grads(ref, first, pieces):
    return jnp.concatenate(
        [ref[(first + i) * E : (first + i + 1) * E, :].astype(f32) for i in range(pieces)], axis=1
    )


def halve_kernel(bit_ref, keep_ref, got_ref, next_keep_ref, next_give_ref):
    half = next_keep_ref.shape[0]
    bit = bit_ref[0]
    for part, ref in ((bit, next_keep_ref), (1 - bit, next_give_ref)):
        rows = pl.ds(pl.multiple_of(part * half, 128), half)
        ref[...] = (keep_ref[rows, :].astype(f32) + got_ref[rows, :].astype(f32)).astype(bf16)


def ride_kernel(keep_ref, got_ref, one_ref, earlier_ref, out_ref):
    cut = one_ref.shape[1]
    total = (keep_ref[...].astype(f32) + got_ref[...].astype(f32)).astype(bf16)
    out_ref[:, :cut, :] = one_ref[...]
    out_ref[:, cut:, :] = total.reshape(out_ref.shape[0], out_ref.shape[1] - cut, 128)


def ride_back_kernel(back_ref, two_ref, out_ref):
    cut = two_ref.shape[1]
    total = jnp.sum(back_ref[:, cut:, :].astype(f32), axis=0).astype(bf16)
    out_ref[:, :cut, :] = two_ref[...]
    out_ref[:, cut:, :] = jnp.broadcast_to(total[None], out_ref[:, cut:, :].shape)


def share_kernel(back_ref, zero_ref, one_ref, out_ref):
    pieces = out_ref.shape[1] // back_ref.shape[0]
    share = back_ref[:, back_ref.shape[1] - pieces :, :].reshape(out_ref.shape[1], 128)
    out_ref[...] = jnp.broadcast_to(share[None], out_ref.shape)


def unpack_kernel(
    core_ref, mine_ref, got_ref, query_ref, key_ref, value_ref, w_out_ref, up_ref, down_t_ref, all_ref
):
    chips, share, _ = mine_ref.shape
    core = core_ref[0]
    for half, ref in ((core, mine_ref), (1 - core, got_ref)):
        for chip in range(chips):
            place = (chip % 2) * 2 + chip // 2
            start = pl.multiple_of(half * (chips * share) + place * share, 128)
            all_ref[pl.ds(start, share), :] = ref[chip]
    for i, ref in enumerate((query_ref, key_ref, value_ref, w_out_ref)):
        ref[...] = take_grads(all_ref, 2 * i, 2)[:, :E]
    up_ref[...] = take_grads(all_ref, 8, 6)
    down_t_ref[...] = take_grads(all_ref, 14, 6)


def vmem_specs(n):
    return [pl.BlockSpec(memory_space=pltpu.VMEM)] * n


SMEM_SPEC = pl.BlockSpec(memory_space=pltpu.SMEM)
MIB = 1024 * 1024


BUSY = pl.CostEstimate(flops=10**9, bytes_accessed=4 * MIB, transcendentals=0)
ANY_SPEC = pl.BlockSpec(memory_space=pl.ANY)
HBM_SPEC = pl.BlockSpec(memory_space=pltpu.HBM)
PARAMS = pltpu.CompilerParams(vmem_limit_bytes=12 * MIB)
BIG_PARAMS = pltpu.CompilerParams(vmem_limit_bytes=62 * MIB)


def shape(dims, dtype=bf16):
    return jax.ShapeDtypeStruct(dims, dtype)


def small_call(kernel, out_shape, *args, scalars=(), scratch=(), cost=None):
    return pl.pallas_call(
        kernel,
        out_shape=out_shape,
        in_specs=[SMEM_SPEC] * len(scalars) + vmem_specs(len(args)),
        out_specs=jax.tree.map(lambda _: vmem_specs(1)[0], out_shape),
        scratch_shapes=scratch,
        compiler_params=PARAMS,
        cost_estimate=cost,
    )(*scalars, *args)


def prepare(asked, test_cells, cotangent, weights):
    w_query, q_gain, w_key, k_gain, w_value, w_out, gain_one, w_up, w_down, gain_two = weights
    rows, wide = test_cells.shape
    ht = H * rows
    shapes = (
        shape((4, 2, W, W)),
        shape((W, 2 * FFH + W)),
        shape((4, W), f32),
        shape((2, 2 * rows, W), f32),
        shape((2, W, ht)),
    )
    args = (test_cells, cotangent, w_query, w_key, w_value, w_out, w_up, w_down.T) + tuple(
        gain.reshape(1, E) for gain in (q_gain, k_gain, gain_one, gain_two)
    )
    return small_call(prepare_kernel, shapes, *args, scalars=(asked,))


def main_call(source, owner_of, core, rec, prepared, rows, tile):
    count = owner_of.shape[0]
    keys = count * BLK
    owners, _, wide = rec.shape
    ht = H * rows
    return pl.pallas_call(
        functools.partial(main_kernel, tile),
        out_shape=(
            shape((rows, wide)),
            shape((rows, wide)),
            pltpu.HBM((owners, 96, 128), bf16),
            pltpu.HBM((owners, 48, 128), bf16),
            pltpu.HBM((owners, 48, 128), bf16),
            pltpu.HBM((GRAD_ROWS // 2, 128), bf16),
            pltpu.HBM((GRAD_ROWS // 2, 128), bf16),
        ),
        in_specs=[SMEM_SPEC] * 3 + [HBM_SPEC] * (1 + len(prepared)),
        out_specs=tuple(vmem_specs(2)) + (HBM_SPEC,) * 5,
        scratch_shapes=[pltpu.VMEM(x.shape, x.dtype) for x in prepared]
        + [
            pltpu.VMEM((keys, wide), bf16),
            pltpu.VMEM((2, keys, W), f32),
            pltpu.VMEM((2, keys, W), bf16),
            pltpu.VMEM((2, keys, W), bf16),
            pltpu.VMEM((2, keys, ht), f32),
            pltpu.VMEM((2, keys, ht), bf16),
            pltpu.VMEM((2, keys, ht), bf16),
            pltpu.VMEM((keys, 4 * W), bf16),
            pltpu.VMEM((GRAD_ROWS, 128), bf16),
            pltpu.VMEM((owners, 96, 128), bf16),
            pltpu.VMEM((owners, 48, 128), bf16),
            pltpu.VMEM((owners, 48, 128), bf16),
            pltpu.SemaphoreType.DMA,
            pltpu.SemaphoreType.DMA((len(prepared),)),
        ],
        compiler_params=BIG_PARAMS,
    )(source, owner_of, core, rec, *prepared)


def swap(x, axis):
    return lax.all_to_all(x, axis, split_axis=0, concat_axis=0, tiled=True)


def mirror_pairs(owners, groups):
    pairs = []
    for row in range(owners):
        for feat in range(groups):
            z = row % Z
            mirror = row - z + (7 + 4 * (feat % 2) - z) % Z
            pairs.append((row * groups + feat, mirror * groups + feat))
    return pairs


def half_rings(owners, groups):
    return [
        [
            (y * Z + (4 * half + place + 2 * (feat % 2)) % Z) * groups + feat
            for y in range(owners // Z)
            for place in range(4)
        ]
        for feat in range(groups)
        for half in range(2)
    ]


def on_device(
    test_cells,
    train_cells,
    train_present,
    retrieved,
    w_query,
    q_gain,
    w_key,
    k_gain,
    w_value,
    w_out,
    gain_one,
    w_up,
    w_down,
    gain_two,
    cotangent,
):
    owners, groups = lax.axis_size("rows"), lax.axis_size("feat")
    blocks_own = train_cells.shape[0] // BLK
    rows, wide = test_cells.shape
    count = retrieved.shape[1]
    owner_of = retrieved[0] // blocks_own
    me = lax.axis_index("rows")
    feat = lax.axis_index("feat")
    core, low, high = ((feat // bit % 2).reshape(1) for bit in (1, 2, 4))

    marked, requests = pl.pallas_call(
        mark_kernel,
        out_shape=(shape((blocks_own, BLK, wide)), shape((owners, 1, count), jnp.int32)),
        in_specs=[HBM_SPEC] * 3,
        out_specs=tuple(vmem_specs(2)),
        scratch_shapes=[
            pltpu.VMEM(x.shape, x.dtype) for x in (train_cells, train_present, retrieved)
        ]
        + [pltpu.SemaphoreType.DMA((3,))],
        compiler_params=BIG_PARAMS,
    )(train_cells, train_present, retrieved)
    mirrored = lax.ppermute(marked, ("rows", "feat"), mirror_pairs(owners, groups))
    mirrored = pl.pallas_call(
        arrived_kernel,
        out_shape=shape(mirrored.shape),
        in_specs=[ANY_SPEC],
        out_specs=ANY_SPEC,
        input_output_aliases={0: 0},
        compiler_params=PARAMS,
        cost_estimate=BUSY,
    )(mirrored)
    served = jnp.stack([me, me - me % Z + (7 + 4 * core[0] - me % Z) % Z])
    asked_both = pl.pallas_call(
        functools.partial(asked_kernel, blocks_own),
        out_shape=shape((owners, 2), jnp.int32),
        in_specs=[SMEM_SPEC] + vmem_specs(1) + [ANY_SPEC],
        out_specs=vmem_specs(1)[0],
        compiler_params=PARAMS,
    )(served, swap(requests, "rows"), mirrored)
    asked = asked_both[:, 0]
    half = (me % Z - 2 * core[0]) % Z // 4
    to_send = pl.pallas_call(
        pick_kernel,
        out_shape=shape((owners // 2, 2, BLK, wide)),
        in_specs=[SMEM_SPEC] * 2 + [ANY_SPEC] * 2,
        out_specs=ANY_SPEC,
        scratch_shapes=[pltpu.SemaphoreType.DMA],
        compiler_params=PARAMS,
    )(asked_both, (half * 4 + 2 * core[0]).reshape(1), marked, mirrored)
    rec = lax.all_to_all(
        to_send.reshape(owners // 2, 2 * BLK, wide),
        ("rows", "feat"),
        split_axis=0,
        concat_axis=0,
        tiled=True,
        axis_index_groups=half_rings(owners, groups),
    ).reshape(owners, BLK, wide)
    place = (owner_of % Z - 2 * core[0]) % Z
    near = place // 4 == half
    source = (owner_of // Z * 4 + jnp.where(near, place, 7 - place) % 4) * 2 + jnp.where(near, 0, 1)
    prepared = prepare(
        asked,
        test_cells,
        cotangent,
        (w_query, q_gain, w_key, k_gain, w_value, w_out, gain_one, w_up, w_down, gain_two),
    )
    out_cells, grad_test, zero, one, two, keep, give = main_call(
        source, owner_of, core, rec, prepared, rows, 1024
    )

    back_zero = swap(zero, "rows")
    got = flip(give, 1)
    half = keep.shape[0] // 2
    keep, give = small_call(halve_kernel, (shape((half, 128)),) * 2, keep, got, scalars=(low,))
    got = flip(give, 2)
    half = half // 2
    keep, give = small_call(halve_kernel, (shape((half, 128)),) * 2, keep, got, scalars=(high,))
    got = flip(give, 4)
    piece = half // owners
    riding = shape((owners, one.shape[1] + piece, 128))
    ride = pl.pallas_call(
        ride_kernel,
        out_shape=riding,
        in_specs=vmem_specs(3) + [ANY_SPEC],
        out_specs=vmem_specs(1)[0],
        compiler_params=PARAMS,
    )(keep, got, one, back_zero)
    back_one = swap(ride, "rows")
    back_two = swap(small_call(ride_back_kernel, riding, back_one, two), "rows")
    chips = groups // 2
    sums = small_call(
        sum_kernel,
        tuple(shape((blocks_own, x.shape[1], 128), f32) for x in (zero, one)),
        back_zero,
        back_one,
        scalars=(asked,),
        cost=BUSY,
    )
    copies = pl.pallas_call(
        share_kernel,
        out_shape=shape((chips, half, 128)),
        in_specs=vmem_specs(1) + [ANY_SPEC] * 2,
        out_specs=vmem_specs(1)[0],
        compiler_params=PARAMS,
    )(back_two, *sums)
    mine = lax.all_to_all(
        copies,
        "feat",
        split_axis=0,
        concat_axis=0,
        tiled=True,
        axis_index_groups=[[2 * chip + c for chip in range(chips)] for c in range(2)],
    )
    others = flip(mine, 1)
    grad_train = small_call(
        last_kernel,
        shape((blocks_own, BLK, wide)),
        *sums,
        back_two,
        scalars=(asked,),
        scratch=[pltpu.VMEM((blocks_own, two.shape[1], 128), f32)],
        cost=BUSY,
    ).reshape(blocks_own * BLK, wide)
    *weights, g_down_t = unpack(core, mine, others)
    return (out_cells, grad_test, grad_train, *weights, g_down_t.T)


def flip(x, bit):
    count = lax.axis_size("feat")
    return lax.ppermute(x, "feat", [(i, i ^ bit) for i in range(count)])


def unpack(core, mine, others):
    return small_call(
        unpack_kernel,
        (shape((E, E), f32),) * 4 + (shape((E, FFH), f32),) * 2,
        mine,
        others,
        scalars=(core,),
        scratch=[pltpu.VMEM((GRAD_ROWS, 128), bf16)],
    )


def solution(mesh):
    in_specs = (
        P("rows", "feat"),
        P("rows", "feat"),
        P("feat", "rows"),
        P("rows", None),
        P(),
        P(),
        P(),
        P(),
        P(),
        P(),
        P(),
        P(),
        P(),
        P(),
        P("rows", "feat"),
    )
    out_specs = (
        P("rows", "feat"),
        P("rows", "feat"),
        P("rows", "feat"),
        P(),
        P(),
        P(),
        P(),
        P(),
        P(),
    )
    return jax.shard_map(
        on_device, mesh=mesh, in_specs=in_specs, out_specs=out_specs, check_vma=False
    )
```

```python
import functools
import math

import jax
import jax.numpy as jnp
from jax import lax
from jax.experimental import pallas as pl
from jax.experimental.pallas import tpu as pltpu
from jax.sharding import PartitionSpec as P

H = 6
BLK = 64
E = 192
W = 256
FFH = 768
SIZE = E // H
TEMPER = 1.5 / math.sqrt(SIZE)
LOG2E = math.log2(math.e)
GELU_C = math.sqrt(2.0 / math.pi)
ABSENT = 8.0
ABSENT_ABOVE = 7.0
MASKED = -30000.0
GRAD_ROWS = 4096
Z = 8

bf16 = jnp.bfloat16
f32 = jnp.float32


def dot_nn(a, b):
    return lax.dot_general(a, b, (((1,), (0,)), ((), ())), preferred_element_type=f32)


def dot_nt(a, b):
    return lax.dot_general(a, b, (((1,), (1,)), ((), ())), preferred_element_type=f32)


def dot_tn(a, b):
    return lax.dot_general(a, b, (((0,), (0,)), ((), ())), preferred_element_type=f32)


def mark_kernel(
    train_hbm,
    present_hbm,
    retrieved_hbm,
    marked_ref,
    requests_ref,
    train_ref,
    present_ref,
    retrieved_ref,
    sems,
):
    copies = [
        pltpu.make_async_copy(source, target, sems.at[i])
        for i, (source, target) in enumerate(
            ((train_hbm, train_ref), (present_hbm, present_ref), (retrieved_hbm, retrieved_ref))
        )
    ]
    for copy in copies:
        copy.start()
    for copy in copies:
        copy.wait()
    wide = train_ref.shape[1]
    feats, rows = present_ref.shape
    present = jnp.concatenate(
        [present_ref[...].astype(f32), jnp.zeros((16 - feats, rows), f32)], axis=0
    ).astype(bf16)
    feature = lax.broadcasted_iota(jnp.int32, (16, wide), 0)
    lane = lax.broadcasted_iota(jnp.int32, (16, wide), 1)
    mine = (lane >= feature * E) & (lane < (feature + 1) * E)
    mask = dot_tn(present, jnp.where(mine, 1.0, 0.0).astype(bf16))
    marked = jnp.where(mask > 0.5, train_ref[...].astype(f32), ABSENT).astype(bf16)
    marked_ref[...] = marked.reshape(marked_ref.shape)
    requests_ref[...] = jnp.broadcast_to(retrieved_ref[...][None], requests_ref.shape)


def arrived_kernel(in_ref, out_ref):
    pass


def asked_kernel(blocks, served_ref, table_ref, mirrored_ref, out_ref):
    table = table_ref[:, 0, :]
    owner = lax.div(table, blocks)
    wanted = lax.rem(table, blocks) + 1
    part = lax.broadcasted_iota(jnp.int32, out_ref.shape, 1)
    own, mirrored = (
        jnp.sum(jnp.where(owner == served_ref[i], wanted, 0), axis=1, keepdims=True) - 1
        for i in range(2)
    )
    out_ref[...] = jnp.where(part == 0, own, mirrored)


def pick_kernel(asked_ref, base_ref, own_ref, mirrored_ref, out_ref, sem):
    def body(k, carry):
        row = (k // 4) * Z + lax.rem(base_ref[0] + lax.rem(k, 4), Z)
        for part, ref in enumerate((own_ref, mirrored_ref)):
            pltpu.make_async_copy(
                ref.at[jnp.maximum(asked_ref[row, part], 0)], out_ref.at[k, part], sem
            ).start()
        return carry

    lax.fori_loop(0, out_ref.shape[0], body, 0)
    pltpu.make_async_copy(out_ref, out_ref, sem).wait()


def add_terms(asked_ref, back_ref, acc_ref):
    def body(slot, carry):
        asked = asked_ref[slot]

        @pl.when(asked >= 0)
        def _():
            acc_ref[asked] += back_ref[slot, : acc_ref.shape[1]].astype(f32)

        return carry

    lax.fori_loop(0, back_ref.shape[0], body, 0)


def sum_kernel(asked_ref, zero_ref, one_ref, zero_sum, one_sum, zero_acc, one_acc):
    for ref, acc, out in ((zero_ref, zero_acc, zero_sum), (one_ref, one_acc, one_sum)):
        acc[...] = jnp.zeros(acc.shape, f32)
        add_terms(asked_ref, ref, acc)
        out[...] = acc[...].astype(bf16)


def last_kernel(asked_ref, zero_ref, one_ref, back_ref, out_ref, acc_ref):
    acc_ref[...] = jnp.zeros_like(acc_ref)
    add_terms(asked_ref, back_ref, acc_ref)
    out_ref[:, :, 0:128] = zero_ref[:, :BLK]
    out_ref[:, :32, 128:256] = zero_ref[:, BLK:]
    out_ref[:, 32:, 128:256] = one_ref[:, :32]
    out_ref[:, :32, 256:384] = one_ref[:, 32:]
    out_ref[:, 32:, 256:384] = acc_ref[...].astype(bf16)


def mean_e(x):
    return jnp.sum(x, axis=-1, keepdims=True) * (1.0 / E)


def head_blocks(full):
    return jnp.concatenate(
        [full[SIZE * h : SIZE * (h + 1), 128 * h : 128 * (h + 1)] for h in range(H)]
        + [jnp.zeros((W - E, 128), f32)],
        axis=0,
    )


def spread_columns(tall, last):
    row = lax.broadcasted_iota(jnp.int32, tall.shape, 0)
    parts = []
    for h in range(H):
        inside = (row >= SIZE * h) & (row < SIZE * (h + 1))
        part = jnp.where(inside, tall, 0.0)
        if last:
            part = jnp.where(row == E, 1.0, part)
        parts.append(part)
    return jnp.concatenate(parts, axis=1).astype(bf16)


def spread_rows(wide):
    lane = lax.broadcasted_iota(jnp.int32, wide.shape, 1)
    parts = []
    for h in range(H):
        inside = (lane >= SIZE * h) & (lane < SIZE * (h + 1))
        parts.append(jnp.where(inside, wide, 0.0))
    return jnp.concatenate(parts, axis=0).astype(bf16)


def layer_norm(x, lane_in):
    centred = jnp.where(lane_in, x - mean_e(x), 0.0)
    scale = lax.rsqrt(mean_e(centred * centred) + 1e-05)
    return centred * scale, scale


def layer_norm_back(hat, scale, gain, dy):
    u = dy * gain
    return scale * (u - mean_e(u) - hat * mean_e(u * hat))


def rms_back(pre, scale, gain, dy):
    u = dy * gain
    return scale * (u - pre * (scale * scale) * mean_e(pre * u))


def feature_lanes(f):
    return slice(128 * f, 128 * f + W)


def side_by_side(first, second):
    return jnp.concatenate(
        [first[:, :128], first[:, 128:] + second[:, :128], second[:, 128:]], axis=1
    )


def widen(x, cols):
    return jnp.concatenate([x, jnp.zeros((x.shape[0], cols - x.shape[1]), x.dtype)], axis=1)


def heighten(x, rows):
    return jnp.concatenate([x, jnp.zeros((rows - x.shape[0], x.shape[1]), x.dtype)], axis=0)


def prepare_kernel(
    asked_ref,
    test_ref,
    cot_ref,
    w_query_ref,
    w_key_ref,
    w_value_ref,
    w_out_ref,
    w_up_ref,
    w_down_t_ref,
    q_gain_ref,
    k_gain_ref,
    gain_one_ref,
    gain_two_ref,
    projections_ref,
    ffn_ref,
    gains_ref,
    cells_ref,
    q_tall_ref,
):
    rows = test_ref.shape[0]
    row = lax.broadcasted_iota(jnp.int32, (E, W), 0)
    lane = lax.broadcasted_iota(jnp.int32, (E, W), 1)
    place = jnp.where(row == lane, 1.0, 0.0).astype(bf16)
    first = jnp.where((row == 0) & (lane == E), 1.0, 0.0).astype(bf16)
    nothing = jnp.zeros((W - E, W), bf16)
    weights = (
        widen(w_query_ref[...], W),
        widen(w_key_ref[...], W) + first,
        widen(w_value_ref[...], W),
        place,
    )
    for i, weight in enumerate(weights):
        for f in range(2):
            skip = f * (W - E)
            projections_ref[i, f, skip : skip + E, :] = weight
            projections_ref[i, f, (1 - f) * E : (1 - f) * E + W - E, :] = nothing
    ffn_ref[:, :FFH] = heighten(w_up_ref[...], W)
    ffn_ref[:, FFH : 2 * FFH] = heighten(w_down_t_ref[...], W)
    ffn_ref[:, 2 * FFH :] = heighten(widen(w_out_ref[...], W), W)
    for i, ref in enumerate((q_gain_ref, k_gain_ref, gain_one_ref, gain_two_ref)):
        gains_ref[i : i + 1, :] = widen(ref[...], W)
    test = test_ref[...]
    cot = cot_ref[...]
    q_gain = gains_ref[0:1, :]
    for f in range(2):
        here = slice(f * rows, (f + 1) * rows)
        lanes = feature_lanes(f)
        cells_ref[0, here, :] = dot_nn(test[:, lanes], projections_ref[3, f])
        cells_ref[1, here, :] = dot_nn(cot[:, lanes], projections_ref[3, f])
        pre = dot_nn(test[:, lanes], projections_ref[0, f])
        norm = pre * lax.rsqrt(mean_e(pre * pre) + 1e-06) * q_gain
        norm = norm.astype(bf16).astype(f32)
        q_tall_ref[f] = spread_columns(norm.T, True)


def main_kernel(
    tile,
    source_ref,
    owner_ref,
    core_ref,
    rec_hbm,
    projections_hbm,
    ffn_hbm,
    gains_hbm,
    cells_hbm,
    q_tall_hbm,
    out_ref,
    grad_test_ref,
    zero_hbm,
    one_hbm,
    two_hbm,
    keep_hbm,
    give_hbm,
    projections_ref,
    ffn_ref,
    gains_ref,
    cells_ref,
    q_tall_ref,
    cells_s,
    kp_s,
    k_s,
    v_s,
    e_s,
    p_s,
    ds_s,
    d_s,
    grads_ref,
    zero_ref,
    one_ref,
    two_ref,
    rec_sem,
    sems,
):
    count = owner_ref.shape[0]
    feats = 2
    rows = out_ref.shape[0]
    keys = count * BLK

    def gather(j, carry):
        pltpu.make_async_copy(
            rec_hbm.at[source_ref[j]],
            cells_s.at[pl.ds(pl.multiple_of(j * BLK, BLK), BLK), :],
            rec_sem,
        ).start()
        return carry

    lax.fori_loop(0, count, gather, 0)
    copies = [
        pltpu.make_async_copy(source, target, sems.at[i])
        for i, (source, target) in enumerate(
            (
                (projections_hbm, projections_ref),
                (gains_hbm, gains_ref),
                (q_tall_hbm, q_tall_ref),
                (cells_hbm, cells_ref),
                (ffn_hbm, ffn_ref),
            )
        )
    ]
    for copy in copies:
        copy.start()
    zero_ref[...] = jnp.zeros_like(zero_ref)
    one_ref[...] = jnp.zeros_like(one_ref)
    two_ref[...] = jnp.zeros_like(two_ref)
    pltpu.make_async_copy(cells_s, cells_s, rec_sem).wait()
    for copy in copies[:3]:
        copy.wait()

    q_gain = gains_ref[0:1, :]
    k_gain = gains_ref[1:2, :]
    gain_one = gains_ref[2:3, :]
    gain_two = gains_ref[3:4, :]

    tiles = [slice(t * tile, (t + 1) * tile) for t in range(keys // tile)]
    totals = []
    for f in range(feats):
        total = jnp.zeros((8, H * rows), f32)
        for here in tiles:
            cells = cells_s[here, feature_lanes(f)]
            pre = dot_nn(cells, projections_ref[1, f])
            lane = lax.broadcasted_iota(jnp.int32, pre.shape, 1)
            body = jnp.where(lane < E, pre, 0.0)
            scale = lax.rsqrt(mean_e(body * body) + 1e-06)
            bias = jnp.where((lane == E) & (pre > ABSENT_ABOVE), MASKED, 0.0)
            norm = (body * scale * k_gain + bias).astype(bf16)
            kp_s[f, here, :] = body
            k_s[f, here, :] = norm
            v_s[f, here, :] = dot_nn(cells, projections_ref[2, f]).astype(bf16)
            e = jnp.exp2(dot_nn(norm, q_tall_ref[f]) * (TEMPER * LOG2E))
            e_s[f, here, :] = e
            total = total + jnp.sum(e.reshape(tile // 8, 8, H * rows), axis=0)
        totals.append(jnp.sum(total, axis=0, keepdims=True))
    inverse = [1.0 / total for total in totals]
    inverse_tempered = [TEMPER / total for total in totals]
    mixed = []
    for f in range(feats):
        for here in tiles:
            p_s[f, here, :] = (e_s[f, here, :] * inverse[f]).astype(bf16)
        mixed.append(dot_tn(v_s[f, :, :E], p_s[f]))
    attended_t = [head_blocks(m) for m in mixed]

    for copy in copies[3:]:
        copy.wait()
    attended = jnp.concatenate([a.T for a in attended_t], axis=0).astype(bf16)
    lane_in = lax.broadcasted_iota(jnp.int32, (feats * rows, W), 1) < E
    w_up = ffn_ref[:, :FFH]
    w_down_t = ffn_ref[:, FFH : 2 * FFH]
    w_out = ffn_ref[:, 2 * FFH :]
    inner_one = cells_ref[0] + dot_nn(attended, w_out)
    hat_one, scale_one = layer_norm(inner_one, lane_in)
    normed_one = (hat_one * gain_one).astype(bf16)
    pre = dot_nn(normed_one, w_up)
    tanh = jnp.tanh(GELU_C * (pre + 0.044715 * (pre * pre * pre)))
    hidden = (0.5 * pre * (1.0 + tanh)).astype(bf16)
    slope = 0.5 * (1.0 + tanh) + (0.5 * GELU_C) * pre * (1.0 - tanh * tanh) * (
        1.0 + (3 * 0.044715) * (pre * pre)
    )
    inner_two = normed_one.astype(f32) + dot_nt(hidden, w_down_t)
    hat_two, scale_two = layer_norm(inner_two, lane_in)
    out = (hat_two * gain_two).astype(bf16)
    out_ref[...] = side_by_side(
        dot_nt(out[:rows], projections_ref[3, 0]), dot_nt(out[rows:], projections_ref[3, 1])
    ).astype(bf16)
    d_two = layer_norm_back(hat_two, scale_two, gain_two, cells_ref[1])
    d_two = jnp.where(lane_in, d_two, 0.0)
    d_two_b = d_two.astype(bf16)
    d_pre_b = (dot_nn(d_two_b, w_down_t) * slope).astype(bf16)
    d_normed = d_two + dot_nt(d_pre_b, w_up)
    d_one = layer_norm_back(hat_one, scale_one, gain_one, d_normed)
    d_one = jnp.where(lane_in, d_one, 0.0)
    d_one_b = d_one.astype(bf16)
    d_att = dot_nt(d_one_b, w_out).astype(bf16).astype(f32)
    put_grads(grads_ref, 6, dot_tn(attended, d_one_b)[:E])
    put_grads(grads_ref, 8, dot_tn(normed_one, d_pre_b)[:E])
    put_grads(grads_ref, 14, dot_tn(d_two_b, hidden)[:E])

    da_t, da_rows, dots = [], [], []
    q_cells, q_pre, q_scale, q_rows = [], [], [], []
    for f in range(feats):
        cells = cells_ref[0, f * rows : (f + 1) * rows, :].astype(bf16)
        pre = dot_nn(cells, projections_ref[0, 0])
        scale = lax.rsqrt(mean_e(pre * pre) + 1e-06)
        q_cells.append(cells)
        q_pre.append(pre)
        q_scale.append(scale)
        q_rows.append(spread_rows((pre * scale * q_gain).astype(bf16).astype(f32)))
        mine = d_att[f * rows : (f + 1) * rows]
        mine_t = mine.T
        da_t.append(spread_columns(mine_t, False))
        da_rows.append(spread_rows(mine))
        product = mine_t * attended_t[f]
        dots.append(
            jnp.concatenate(
                [
                    jnp.sum(product[SIZE * h : SIZE * (h + 1)], axis=0, keepdims=True)
                    for h in range(H)
                ],
                axis=1,
            )
        )

    d_queries = []
    for f in range(feats):
        for here in tiles:
            grad_w = dot_nn(v_s[f, here, :], da_t[f])
            probs = e_s[f, here, :] * inverse_tempered[f]
            ds_s[f, here, :] = (probs * (grad_w - dots[f])).astype(bf16)
        d_queries.append(dot_tn(k_s[f, :, :E], ds_s[f]))
    for t, here in enumerate(tiles):
        d_cells = []
        for f in range(feats):
            d_key = dot_nn(ds_s[f, here, :], q_rows[f])
            d_value = dot_nn(p_s[f, here, :], da_rows[f]).astype(bf16)
            body = kp_s[f, here, :]
            scale = lax.rsqrt(mean_e(body * body) + 1e-06)
            d_kpre = rms_back(body, scale, k_gain, d_key).astype(bf16)
            d_s[here, 2 * f * W : (2 * f + 1) * W] = d_kpre
            d_s[here, (2 * f + 1) * W : (2 * f + 2) * W] = d_value
            d_cells.append(
                dot_nt(d_kpre, projections_ref[1, f]) + dot_nt(d_value, projections_ref[2, f])
            )
        d_cells = side_by_side(*d_cells).astype(bf16)
        for b in range(tile // BLK):
            owner = owner_ref[t * (tile // BLK) + b]
            block = d_cells[b * BLK : (b + 1) * BLK]
            zero_ref[owner, :BLK] = block[:, :128]
            zero_ref[owner, BLK:] = block[:32, 128:256]
            one_ref[owner, :32] = block[32:, 128:256]
            one_ref[owner, 32:] = block[:32, 256:]
            two_ref[owner] = block[32:, 256:]

    sends = [
        pltpu.make_async_copy(source, target, sems.at[i])
        for i, (source, target) in enumerate(
            ((zero_ref, zero_hbm), (one_ref, one_hbm), (two_ref, two_hbm))
        )
    ]
    for copy in sends:
        copy.start()

    d_test = []
    g_query = jnp.zeros((W, W), f32)
    placed = []
    for f in range(feats):
        here = slice(f * rows, (f + 1) * rows)
        d_query = head_blocks(d_queries[f]).T
        d_qpre = rms_back(q_pre[f], q_scale[f], q_gain, d_query).astype(bf16)
        g_query = g_query + dot_tn(q_cells[f], d_qpre)
        d_test.append(dot_nt(d_qpre, projections_ref[0, f]))
        placed.append(d_one[here, :E])
    grad_test_ref[...] = (side_by_side(*d_test) + jnp.concatenate(placed, axis=1)).astype(bf16)
    put_grads(grads_ref, 0, g_query[:E])
    kv = jnp.zeros((E, 2 * W), f32)
    for f in range(feats):
        both = dot_tn(cells_s[:, feature_lanes(f)], d_s[:, 2 * f * W : 2 * (f + 1) * W])
        kv = kv + both[f * (W - E) : f * (W - E) + E]
    put_grads(grads_ref, 2, kv)
    grads_ref[20 * E :, :] = jnp.zeros((GRAD_ROWS - 20 * E, 128), bf16)
    core = core_ref[0]
    for i, (half, target) in enumerate(((core, keep_hbm), (1 - core, give_hbm))):
        start = pl.multiple_of(half * (GRAD_ROWS // 2), 128)
        copy = pltpu.make_async_copy(
            grads_ref.at[pl.ds(start, GRAD_ROWS // 2), :], target, sems.at[len(sends)]
        )
        copy.start()
        sends.append(copy)
    for copy in sends:
        copy.wait()


def put_grads(grads_ref, first, value):
    for i in range(value.shape[1] // 128):
        rows = slice((first + i) * E, (first + i + 1) * E)
        grads_ref[rows, :] = value[:, 128 * i : 128 * (i + 1)].astype(bf16)


def take_grads(ref, first, pieces):
    return jnp.concatenate(
        [ref[(first + i) * E : (first + i + 1) * E, :].astype(f32) for i in range(pieces)], axis=1
    )


def halve_kernel(bit_ref, keep_ref, got_ref, next_keep_ref, next_give_ref):
    half = next_keep_ref.shape[0]
    bit = bit_ref[0]
    for part, ref in ((bit, next_keep_ref), (1 - bit, next_give_ref)):
        rows = pl.ds(pl.multiple_of(part * half, 128), half)
        ref[...] = (keep_ref[rows, :].astype(f32) + got_ref[rows, :].astype(f32)).astype(bf16)


def ride_kernel(keep_ref, got_ref, one_ref, earlier_ref, out_ref):
    cut = one_ref.shape[1]
    total = (keep_ref[...].astype(f32) + got_ref[...].astype(f32)).astype(bf16)
    out_ref[:, :cut, :] = one_ref[...]
    out_ref[:, cut:, :] = total.reshape(out_ref.shape[0], out_ref.shape[1] - cut, 128)


def ride_back_kernel(back_ref, two_ref, out_ref):
    cut = two_ref.shape[1]
    pieces = out_ref.shape[1] - cut
    total = jnp.sum(back_ref[:, back_ref.shape[1] - pieces :, :].astype(f32), axis=0).astype(bf16)
    out_ref[:, :cut, :] = two_ref[...]
    out_ref[:, cut:, :] = jnp.broadcast_to(total[None], out_ref[:, cut:, :].shape)


def share_kernel(back_ref, zero_ref, one_ref, out_ref):
    pieces = out_ref.shape[1] // back_ref.shape[0]
    share = back_ref[:, back_ref.shape[1] - pieces :, :].reshape(out_ref.shape[1], 128)
    out_ref[...] = jnp.broadcast_to(share[None], out_ref.shape)


def unpack_kernel(
    core_ref, mine_ref, got_ref, query_ref, key_ref, value_ref, w_out_ref, up_ref, down_t_ref, all_ref
):
    chips, share, _ = mine_ref.shape
    core = core_ref[0]
    for half, ref in ((core, mine_ref), (1 - core, got_ref)):
        for chip in range(chips):
            place = (chip % 2) * 2 + chip // 2
            start = pl.multiple_of(half * (chips * share) + place * share, 128)
            all_ref[pl.ds(start, share), :] = ref[chip]
    for i, ref in enumerate((query_ref, key_ref, value_ref, w_out_ref)):
        ref[...] = take_grads(all_ref, 2 * i, 2)[:, :E]
    up_ref[...] = take_grads(all_ref, 8, 6)
    down_t_ref[...] = take_grads(all_ref, 14, 6)


def vmem_specs(n):
    return [pl.BlockSpec(memory_space=pltpu.VMEM)] * n


SMEM_SPEC = pl.BlockSpec(memory_space=pltpu.SMEM)
MIB = 1024 * 1024


BUSY = pl.CostEstimate(flops=10**9, bytes_accessed=4 * MIB, transcendentals=0)
ANY_SPEC = pl.BlockSpec(memory_space=pl.ANY)
HBM_SPEC = pl.BlockSpec(memory_space=pltpu.HBM)
PARAMS = pltpu.CompilerParams(vmem_limit_bytes=12 * MIB)
BIG_PARAMS = pltpu.CompilerParams(vmem_limit_bytes=62 * MIB)


def shape(dims, dtype=bf16):
    return jax.ShapeDtypeStruct(dims, dtype)


def small_call(kernel, out_shape, *args, scalars=(), scratch=(), cost=None):
    return pl.pallas_call(
        kernel,
        out_shape=out_shape,
        in_specs=[SMEM_SPEC] * len(scalars) + vmem_specs(len(args)),
        out_specs=jax.tree.map(lambda _: vmem_specs(1)[0], out_shape),
        scratch_shapes=scratch,
        compiler_params=PARAMS,
        cost_estimate=cost,
    )(*scalars, *args)


def prepare(asked, test_cells, cotangent, weights):
    w_query, q_gain, w_key, k_gain, w_value, w_out, gain_one, w_up, w_down, gain_two = weights
    rows, wide = test_cells.shape
    ht = H * rows
    shapes = (
        shape((4, 2, W, W)),
        shape((W, 2 * FFH + W)),
        shape((4, W), f32),
        shape((2, 2 * rows, W), f32),
        shape((2, W, ht)),
    )
    args = (test_cells, cotangent, w_query, w_key, w_value, w_out, w_up, w_down.T) + tuple(
        gain.reshape(1, E) for gain in (q_gain, k_gain, gain_one, gain_two)
    )
    return small_call(prepare_kernel, shapes, *args, scalars=(asked,))


def main_call(source, owner_of, core, rec, prepared, rows, tile):
    count = owner_of.shape[0]
    keys = count * BLK
    owners, _, wide = rec.shape
    ht = H * rows
    return pl.pallas_call(
        functools.partial(main_kernel, tile),
        out_shape=(
            shape((rows, wide)),
            shape((rows, wide)),
            pltpu.HBM((owners, 96, 128), bf16),
            pltpu.HBM((owners, 64, 128), bf16),
            pltpu.HBM((owners, 32, 128), bf16),
            pltpu.HBM((GRAD_ROWS // 2, 128), bf16),
            pltpu.HBM((GRAD_ROWS // 2, 128), bf16),
        ),
        in_specs=[SMEM_SPEC] * 3 + [HBM_SPEC] * (1 + len(prepared)),
        out_specs=tuple(vmem_specs(2)) + (HBM_SPEC,) * 5,
        scratch_shapes=[pltpu.VMEM(x.shape, x.dtype) for x in prepared]
        + [
            pltpu.VMEM((keys, wide), bf16),
            pltpu.VMEM((2, keys, W), f32),
            pltpu.VMEM((2, keys, W), bf16),
            pltpu.VMEM((2, keys, W), bf16),
            pltpu.VMEM((2, keys, ht), f32),
            pltpu.VMEM((2, keys, ht), bf16),
            pltpu.VMEM((2, keys, ht), bf16),
            pltpu.VMEM((keys, 4 * W), bf16),
            pltpu.VMEM((GRAD_ROWS, 128), bf16),
            pltpu.VMEM((owners, 96, 128), bf16),
            pltpu.VMEM((owners, 64, 128), bf16),
            pltpu.VMEM((owners, 32, 128), bf16),
            pltpu.SemaphoreType.DMA,
            pltpu.SemaphoreType.DMA((len(prepared),)),
        ],
        compiler_params=BIG_PARAMS,
    )(source, owner_of, core, rec, *prepared)


def swap(x, axis):
    return lax.all_to_all(x, axis, split_axis=0, concat_axis=0, tiled=True)


def mirror_pairs(owners, groups):
    pairs = []
    for row in range(owners):
        for feat in range(groups):
            z = row % Z
            mirror = row - z + (7 + 4 * (feat % 2) - z) % Z
            pairs.append((row * groups + feat, mirror * groups + feat))
    return pairs


def half_rings(owners, groups):
    return [
        [
            (y * Z + (4 * half + place + 2 * (feat % 2)) % Z) * groups + feat
            for y in range(owners // Z)
            for place in range(4)
        ]
        for feat in range(groups)
        for half in range(2)
    ]


def on_device(
    test_cells,
    train_cells,
    train_present,
    retrieved,
    w_query,
    q_gain,
    w_key,
    k_gain,
    w_value,
    w_out,
    gain_one,
    w_up,
    w_down,
    gain_two,
    cotangent,
):
    owners, groups = lax.axis_size("rows"), lax.axis_size("feat")
    blocks_own = train_cells.shape[0] // BLK
    rows, wide = test_cells.shape
    count = retrieved.shape[1]
    owner_of = retrieved[0] // blocks_own
    me = lax.axis_index("rows")
    feat = lax.axis_index("feat")
    core, low, high = ((feat // bit % 2).reshape(1) for bit in (1, 2, 4))

    marked, requests = pl.pallas_call(
        mark_kernel,
        out_shape=(shape((blocks_own, BLK, wide)), shape((owners, 1, count), jnp.int32)),
        in_specs=[HBM_SPEC] * 3,
        out_specs=tuple(vmem_specs(2)),
        scratch_shapes=[
            pltpu.VMEM(x.shape, x.dtype) for x in (train_cells, train_present, retrieved)
        ]
        + [pltpu.SemaphoreType.DMA((3,))],
        compiler_params=BIG_PARAMS,
    )(train_cells, train_present, retrieved)
    mirrored = lax.ppermute(marked, ("rows", "feat"), mirror_pairs(owners, groups))
    mirrored = pl.pallas_call(
        arrived_kernel,
        out_shape=shape(mirrored.shape),
        in_specs=[ANY_SPEC],
        out_specs=ANY_SPEC,
        input_output_aliases={0: 0},
        compiler_params=PARAMS,
        cost_estimate=BUSY,
    )(mirrored)
    served = jnp.stack([me, me - me % Z + (7 + 4 * core[0] - me % Z) % Z])
    asked_both = pl.pallas_call(
        functools.partial(asked_kernel, blocks_own),
        out_shape=shape((owners, 2), jnp.int32),
        in_specs=[SMEM_SPEC] + vmem_specs(1) + [ANY_SPEC],
        out_specs=vmem_specs(1)[0],
        compiler_params=PARAMS,
    )(served, swap(requests, "rows"), mirrored)
    asked = asked_both[:, 0]
    half = (me % Z - 2 * core[0]) % Z // 4
    to_send = pl.pallas_call(
        pick_kernel,
        out_shape=shape((owners // 2, 2, BLK, wide)),
        in_specs=[SMEM_SPEC] * 2 + [ANY_SPEC] * 2,
        out_specs=ANY_SPEC,
        scratch_shapes=[pltpu.SemaphoreType.DMA],
        compiler_params=PARAMS,
    )(asked_both, (half * 4 + 2 * core[0]).reshape(1), marked, mirrored)
    rec = lax.all_to_all(
        to_send.reshape(owners // 2, 2 * BLK, wide),
        ("rows", "feat"),
        split_axis=0,
        concat_axis=0,
        tiled=True,
        axis_index_groups=half_rings(owners, groups),
    ).reshape(owners, BLK, wide)
    place = (owner_of % Z - 2 * core[0]) % Z
    near = place // 4 == half
    source = (owner_of // Z * 4 + jnp.where(near, place, 7 - place) % 4) * 2 + jnp.where(near, 0, 1)
    prepared = prepare(
        asked,
        test_cells,
        cotangent,
        (w_query, q_gain, w_key, k_gain, w_value, w_out, gain_one, w_up, w_down, gain_two),
    )
    out_cells, grad_test, zero, one, two, keep, give = main_call(
        source, owner_of, core, rec, prepared, rows, 1024
    )

    back_zero = swap(zero, "rows")
    got = flip(give, 1)
    half = keep.shape[0] // 2
    keep, give = small_call(halve_kernel, (shape((half, 128)),) * 2, keep, got, scalars=(low,))
    got = flip(give, 2)
    half = half // 2
    keep, give = small_call(halve_kernel, (shape((half, 128)),) * 2, keep, got, scalars=(high,))
    got = flip(give, 4)
    piece = half // owners
    riding, riding_back = (shape((owners, x.shape[1] + piece, 128)) for x in (one, two))
    ride = pl.pallas_call(
        ride_kernel,
        out_shape=riding,
        in_specs=vmem_specs(3) + [ANY_SPEC],
        out_specs=vmem_specs(1)[0],
        compiler_params=PARAMS,
    )(keep, got, one, back_zero)
    back_one = swap(ride, "rows")
    back_two = swap(small_call(ride_back_kernel, riding_back, back_one, two), "rows")
    chips = groups // 2
    sums = small_call(
        sum_kernel,
        tuple(shape((blocks_own, x.shape[1], 128)) for x in (zero, one)),
        back_zero,
        back_one,
        scalars=(asked,),
        scratch=[pltpu.VMEM((blocks_own, x.shape[1], 128), f32) for x in (zero, one)],
        cost=BUSY,
    )
    copies = pl.pallas_call(
        share_kernel,
        out_shape=shape((chips, half, 128)),
        in_specs=vmem_specs(1) + [ANY_SPEC] * 2,
        out_specs=vmem_specs(1)[0],
        compiler_params=PARAMS,
    )(back_two, *sums)
    mine = lax.all_to_all(
        copies,
        "feat",
        split_axis=0,
        concat_axis=0,
        tiled=True,
        axis_index_groups=[[2 * chip + c for chip in range(chips)] for c in range(2)],
    )
    others = flip(mine, 1)
    grad_train = small_call(
        last_kernel,
        shape((blocks_own, BLK, wide)),
        *sums,
        back_two,
        scalars=(asked,),
        scratch=[pltpu.VMEM((blocks_own, two.shape[1], 128), f32)],
        cost=BUSY,
    ).reshape(blocks_own * BLK, wide)
    *weights, g_down_t = unpack(core, mine, others)
    return (out_cells, grad_test, grad_train, *weights, g_down_t.T)


def flip(x, bit):
    count = lax.axis_size("feat")
    return lax.ppermute(x, "feat", [(i, i ^ bit) for i in range(count)])


def unpack(core, mine, others):
    return small_call(
        unpack_kernel,
        (shape((E, E), f32),) * 4 + (shape((E, FFH), f32),) * 2,
        mine,
        others,
        scalars=(core,),
        scratch=[pltpu.VMEM((GRAD_ROWS, 128), bf16)],
    )


def solution(mesh):
    in_specs = (
        P("rows", "feat"),
        P("rows", "feat"),
        P("feat", "rows"),
        P("rows", None),
        P(),
        P(),
        P(),
        P(),
        P(),
        P(),
        P(),
        P(),
        P(),
        P(),
        P("rows", "feat"),
    )
    out_specs = (
        P("rows", "feat"),
        P("rows", "feat"),
        P("rows", "feat"),
        P(),
        P(),
        P(),
        P(),
        P(),
        P(),
    )
    return jax.shard_map(
        on_device, mesh=mesh, in_specs=in_specs, out_specs=out_specs, check_vma=False
    )
```
